32 devices in a mesh: node: 16 (over z, y, x), local: 2 (over core).
Axes of the slice: x: 2, y: 2, z: 4, core: 2. Of those that a mesh axis runs over, the one named last changes fastest.
Arguments:
- grad_out: bfloat16 [4096, 3584], P(('node', 'local')), may hold values from -6 to 6
- expert_ids: int32 [4096, 8], P(('node', 'local')), may hold values from 0 to 63, as said below
- gate_weights: float32 [4096, 8], P(('node', 'local')), may hold values from 0.05 to 0.35
- saved_hidden: bfloat16 [16, 64, 1024], P('node', None, 'local'), may hold values from -0.59765625 to 0.59765625
- down_weight: bfloat16 [16, 1024, 3584], P('node', 'local'), may hold values from -0.1875 to 0.1875
- second_moment: bfloat16 [16, 1024, 3584], P('node', 'local'), may hold values from 0.0019989014 to 0.25
Outputs:
- gate_weight_gradient: float32 [4096, 8], P(('node', 'local'))
- hidden_grad: bfloat16 [16, 64, 1024], P('node', None, 'local')
- new_weight: bfloat16 [16, 1024, 3584], P('node', 'local')
- new_second: bfloat16 [16, 1024, 3584], P('node', 'local')
The draws below stay inside these ranges and needn't reach their ends.
Inputs may be any that keep to these rules, and one draw needn't show every extreme that they name: `expert_ids`: each row names 8 different experts on at most 4 nodes (node = id // 4), two on each; at most one per row is in flight (id % 4 == 0). Among the rows of one device at most 2 name the in-flight expert of any one node, and in every draw some node receives exactly 2 from every device.
All inputs are finite; a program needn't handle non-finite values.
Results may differ from the reference program's by a relative error of at most 0.0051.
Values may be sent and summed in bfloat16 or wider, within the bound.
A program may use at most 128 MiB of HBM per device.

```python
import math
import jax
import jax.numpy as jnp
from jax import lax

D = 3584
H_WIN = 1024
EXPERTS_PER_HOST = 4
CHOSEN_EXPERTS = 8
MAX_NODES = 4
TOK_DEV = 128
CAP = 2
SLOTS = 64
TOTAL_TOKENS = 4096
N_NODE = 16
N_LOCAL = 2


def draw_expert_ids(key, part):
    device_count = N_NODE * N_LOCAL
    token_count = device_count * TOK_DEV
    keys = jax.random.split(key, 8)
    hot_rank = jax.random.permutation(keys[0], N_NODE)
    hot_nodes = hot_rank < max(N_NODE // 8, 1)
    counts = jax.random.randint(keys[1], (device_count, N_NODE), 0, CAP)
    counts = jnp.where(hot_nodes[None, :], CAP, counts)
    order_key = jax.random.randint(keys[2], (device_count, N_NODE), 0, 1 << 20) * N_NODE + jnp.arange(N_NODE)[None, :]
    order = jnp.argsort(order_key, axis=1)
    ordered = jnp.take_along_axis(counts, order, 1)
    ends = jnp.cumsum(ordered, 1)
    position = jnp.arange(TOK_DEV)
    slot_node = jnp.sum((position[None, :, None] >= ends[:, None, :]).astype(jnp.int32), 2)
    valid = slot_node < N_NODE
    listed = jnp.take_along_axis(order, jnp.minimum(slot_node, N_NODE - 1), 1)
    listed = jnp.where(valid, listed, -1)
    shuffle_key = jax.random.randint(keys[3], (device_count, TOK_DEV), 0, 1 << 20) * TOK_DEV + jnp.arange(TOK_DEV)[None, :]
    shuffle = jnp.argsort(shuffle_key, axis=1)
    hit_node = jnp.take_along_axis(listed, shuffle, 1).reshape(token_count)
    node_score = jax.random.randint(keys[4], (token_count, N_NODE), 0, 1 << 16) * N_NODE + jnp.arange(N_NODE)[None, :]
    node_score = node_score + jnp.where(jnp.arange(N_NODE)[None, :] == hit_node[:, None], 1 << 24, 0)
    scores_top, picked_experts = lax.top_k(node_score, MAX_NODES)
    first_pick = jax.random.randint(keys[5], (token_count, MAX_NODES), 0, EXPERTS_PER_HOST - 1)
    second_pick = jax.random.randint(keys[6], (token_count, MAX_NODES), 0, EXPERTS_PER_HOST - 2)
    slot_first = 1 + first_pick
    slot_second = 1 + (first_pick + 1 + second_pick) % (EXPERTS_PER_HOST - 1)
    is_hit = (jnp.arange(MAX_NODES)[None, :] == 0) & (hit_node[:, None] >= 0)
    slot_first = jnp.where(is_hit, 0, slot_first)
    chosen_ids = jnp.concatenate([picked_experts * EXPERTS_PER_HOST + slot_first, picked_experts * EXPERTS_PER_HOST + slot_second], 1)
    column_key = jax.random.randint(keys[7], (token_count, CHOSEN_EXPERTS), 0, 1 << 16) * CHOSEN_EXPERTS + jnp.arange(CHOSEN_EXPERTS)[None, :]
    chosen_ids = jnp.take_along_axis(chosen_ids, jnp.argsort(column_key, axis=1), 1)
    return chosen_ids.astype(jnp.int32)


def block_scale(stream_key, shape, cuts, least, top_value):
    def one(dim, parts):
        heights = jax.random.uniform(jax.random.fold_in(jax.random.fold_in(stream_key, 6), dim), (parts,), jnp.float32, least / len(cuts), top_value / len(cuts))
        return jnp.repeat(jnp.exp(heights), shape[dim] // parts).reshape((-1,) + (1,) * (len(shape) - dim - 1))

    level = one(*cuts[0])
    for cut in cuts[1:]:
        level = level * one(*cut)
    return level


def centred(own_key, dims, spread, reach, shards=(), kind=jnp.bfloat16):
    drawn = jax.random.normal(own_key, dims, jnp.float32) * spread
    if len(shards) > 0:
        drawn = block_scale(own_key, dims, shards, -0.22, 0.18) * drawn
    return jnp.clip(drawn, min=-reach, max=reach).astype(kind)


def setup_inputs(seed: int = 0) -> dict:
    splits = jax.random.split(jax.random.key(seed), 7)
    return {
        "grad_out": centred(splits[0], (TOTAL_TOKENS, D), 1.0, 6.0, ((0, 32),)),
        "expert_ids": draw_expert_ids(jax.random.fold_in(splits[6], 71), 0),
        "gate_weights": jnp.clip(0.05 + 0.29999999 * jax.random.uniform(splits[2], (TOTAL_TOKENS, CHOSEN_EXPERTS), jnp.float32) ** block_scale(splits[2], (TOTAL_TOKENS, CHOSEN_EXPERTS), ((0, 32),), -0.2, 0.2), 0.05, 0.35),
        "saved_hidden": centred(splits[3], (N_NODE, SLOTS, H_WIN), 0.1, 0.59765625, ((0, 16), (2, 2))),
        "down_weight": centred(splits[4], (N_NODE, H_WIN, D), H_WIN ** -0.5, 0.1875, ((0, 16), (1, 2))),
        "second_moment": jnp.clip(jnp.exp(math.log(0.25) - 4.828863 * jax.random.uniform(splits[5], (N_NODE, H_WIN, D), jnp.float32) ** block_scale(splits[5], (N_NODE, H_WIN, D), ((0, 16), (1, 2)), -0.2, 0.2)), 0.0019989014, 0.25).astype(jnp.bfloat16),
    }


beta_second = 0.95
learn_rate = 0.002
decay_rate = 0.1
epsilon = 1e-08
correct_second = 0.994079470779666

def pack_device(picked_experts, gate_values, grads):
    transit_rows = picked_experts % EXPERTS_PER_HOST == 0
    row_present = jnp.any(transit_rows, 1)
    destination_node = lax.optimization_barrier(jnp.sum(jnp.where(transit_rows, picked_experts // EXPERTS_PER_HOST, 0), 1)).astype(jnp.int32)
    onehot = ((destination_node[:, None] == jnp.arange(N_NODE, dtype=jnp.int32)[None, :]) & row_present[:, None]).astype(jnp.int32)
    within_rank = lax.optimization_barrier(jnp.sum(onehot * (jnp.cumsum(onehot, 0) - 1), 1)).astype(jnp.int32)
    slot_index = destination_node * CAP + within_rank
    expert_location = (jnp.arange(N_NODE * CAP, dtype=jnp.int32)[:, None] == slot_index[None, :]) & row_present[None, :]
    matched_gate = lax.optimization_barrier(jnp.sum(jnp.where(transit_rows, gate_values, 0.0), 1)).astype(jnp.bfloat16)
    departing_rows = jnp.dot(expert_location.astype(jnp.bfloat16), grads, preferred_element_type=jnp.float32).astype(jnp.bfloat16)
    departing_gates = lax.optimization_barrier(jnp.sum(jnp.where(expert_location, matched_gate.astype(jnp.float32)[None, :], 0.0), 1)).astype(jnp.bfloat16)
    return (departing_rows, departing_gates, expert_location, transit_rows)

def reference(grad_out, expert_ids, gate_weights, saved_hidden, down_weight, second_moment):
    device_count = N_NODE * N_LOCAL
    bundled_rows = lax.map(lambda item: pack_device(item[0], item[1], item[2]), (expert_ids.reshape(device_count, TOK_DEV, CHOSEN_EXPERTS), gate_weights.reshape(device_count, TOK_DEV, CHOSEN_EXPERTS), grad_out.reshape(device_count, TOK_DEV, D)))
    departing_rows, departing_gates, expert_location, transit_rows = bundled_rows
    departing_rows = departing_rows.reshape(N_NODE, N_LOCAL, N_NODE, CAP, D)
    departing_gates = departing_gates.reshape(N_NODE, N_LOCAL, N_NODE, CAP)

    def per_node(item):
        node_id, weight_now, second_now, hidden_now = item
        arrived = jnp.take(departing_rows, node_id, axis=2)
        arrived = jnp.transpose(arrived, (1, 0, 2, 3)).reshape(SLOTS, D)
        slot_gates = jnp.transpose(jnp.take(departing_gates, node_id, axis=2), (1, 0, 2)).reshape(SLOTS).astype(jnp.float32)
        unscaled = lax.dot_general(arrived, weight_now, (((1,), (1,)), ((), ())), preferred_element_type=jnp.float32)
        hidden_out = (slot_gates[:, None] * unscaled).astype(jnp.bfloat16)
        slot_score = lax.optimization_barrier(jnp.sum(unscaled * hidden_now.astype(jnp.float32), 1))
        scaled = (slot_gates[:, None] * arrived.astype(jnp.float32)).astype(jnp.bfloat16)
        grad = lax.dot_general(hidden_now, scaled, (((0,), (0,)), ((), ())), preferred_element_type=jnp.float32)
        second_new = beta_second * second_now.astype(jnp.float32) + (1.0 - beta_second) * grad * grad
        weight_f = weight_now.astype(jnp.float32)
        update = grad / (jnp.sqrt(second_new / correct_second) + epsilon) + decay_rate * weight_f
        weight_new = weight_f - learn_rate * update
        return (slot_score, hidden_out, weight_new.astype(jnp.bfloat16), second_new.astype(jnp.bfloat16))
    scores, hidden_grad, new_weight, new_second = lax.map(per_node, (jnp.arange(N_NODE, dtype=jnp.int32), down_weight, second_moment, saved_hidden))
    scores = scores.reshape(N_NODE, N_LOCAL, N_NODE, CAP)
    returned = jnp.transpose(scores, (2, 1, 0, 3)).reshape(device_count, N_NODE * CAP)
    token_gradient = lax.optimization_barrier(jnp.sum(jnp.where(expert_location, returned[:, :, None], 0.0), 1))
    gate_weight_gradient = jnp.where(transit_rows, token_gradient[:, :, None], 0.0).reshape(TOTAL_TOKENS, CHOSEN_EXPERTS)
    return (gate_weight_gradient, hidden_grad, new_weight, new_second)
```

```python
import functools

import jax
import jax.numpy as jnp
from jax import lax
from jax.experimental import pallas as pl
from jax.experimental.pallas import tpu as pltpu
from jax.sharding import PartitionSpec as P

MESH = pl.DeviceIdType.MESH
EXPERTS_PER_HOST = 4
CAP = 2
WIDTH = 256
SLAB = 16
BLOCKS = SLAB // CAP
LANES = 128

beta_second = 0.95
learn_rate = 0.002
decay_rate = 0.1
epsilon = 1e-08
correct_second = 0.994079470779666

f32 = jnp.float32
bf16 = jnp.bfloat16


def dot(a, b, dims=((1,), (0,))):
    return lax.dot_general(a, b, (dims, ((), ())), preferred_element_type=f32)


def iota(shape, axis):
    return lax.broadcasted_iota(jnp.int32, shape, axis)


def kernel(
    nodes, members, plan,
    ids_ref, gates_ref, grad_hbm, hidden_hbm, weight_hbm, second_hbm,
    score_out, hidden_out, weight_out, second_out,
    grads, hidden, weight, second, hidden_t, send, recv, picks, x, scaled, gate,
    unscaled, score_send, score_recv,
    load_sem, send_sem, recv_sem, pass_sem, score_send_sem, score_recv_sem,
):
    n, l = lax.axis_index("node"), lax.axis_index("local")
    devices = nodes * members
    me = l * nodes + n
    tokens = grads.shape[0]
    slots, units = hidden.shape
    group = min(32, devices)

    loads = [
        pltpu.make_async_copy(source, target, load_sem.at[i])
        for i, (source, target) in enumerate(
            ((grad_hbm, grads), (hidden_hbm, hidden), (weight_hbm, weight), (second_hbm, second))
        )
    ]
    for load in loads:
        load.start()

    barrier = pltpu.get_barrier_semaphore()

    def greet(k, carry):
        other = lax.rem(me + k, devices)
        pl.semaphore_signal(
            barrier, inc=1, device_id=(lax.rem(other, nodes), other // nodes), device_id_type=MESH
        )
        return carry

    lax.fori_loop(1, devices, greet, 0)

    ids = ids_ref[...]
    hit = ids % EXPERTS_PER_HOST == 0
    hit_one = jnp.where(hit, 1, 0)
    present = jnp.max(hit_one, 0, keepdims=True)
    dest = jnp.sum(jnp.where(hit, ids // EXPERTS_PER_HOST, 0), 0, keepdims=True)
    dest = jnp.where(present > 0, dest, -1)
    onehot = jnp.where(iota((nodes, tokens), 0) == dest, 1.0, 0.0).astype(f32)
    before = jnp.where(iota((tokens, tokens), 0) < iota((tokens, tokens), 1), 1.0, 0.0)
    earlier = dot(onehot.astype(bf16), before.astype(bf16))
    rank = jnp.sum(onehot * earlier, 0, keepdims=True).astype(jnp.int32)
    key = jnp.where(present > 0, dest * SLAB + rank, -SLAB * CAP)
    matched = jnp.sum(jnp.where(hit, gates_ref[...], 0.0), 0, keepdims=True)
    matched = matched.astype(bf16).astype(f32)

    loads[0].wait()
    place = iota((nodes * SLAB, tokens), 0)

    def pack(q):
        total = jnp.zeros((nodes * SLAB, WIDTH), f32)
        for c, block in enumerate(plan[q]):
            mask = place == key + CAP * c
            if block is None:
                total += dot(
                    jnp.where(mask, matched, 0.0).astype(bf16), jnp.ones((tokens, WIDTH), bf16)
                )
            else:
                total += dot(
                    jnp.where(mask, 1.0, 0.0).astype(bf16),
                    grads[:, block * WIDTH:(block + 1) * WIDTH],
                )
        send[q] = total.astype(bf16).reshape(nodes, SLAB, WIDTH)

    def push(q):
        def one(k, carry):
            other = lax.rem(n + k, nodes)
            pltpu.make_async_remote_copy(
                src_ref=send.at[q, other], dst_ref=recv.at[q, me],
                send_sem=send_sem.at[q], recv_sem=recv_sem.at[q, me],
                device_id=(other, l), device_id_type=MESH,
            ).start()
            return carry

        lax.fori_loop(1, nodes, one, 0)
        recv[q, me] = send[q, n]

    def hand_on(q, source):
        for k in range(1, members):
            pltpu.make_async_remote_copy(
                src_ref=recv.at[q, source], dst_ref=recv.at[q, source],
                send_sem=pass_sem.at[q], recv_sem=recv_sem.at[q, source],
                device_id=(n, lax.rem(l + k, members)), device_id_type=MESH,
            ).start()

    def arrival(q, source):
        return pltpu.make_async_copy(
            recv.at[q, source], recv.at[q, source], recv_sem.at[q, source]
        )

    def gather(q):
        def direct(k, carry):
            source = l * nodes + lax.rem(n + nodes - k, nodes)
            arrival(q, source).wait()
            hand_on(q, source)
            return carry

        lax.fori_loop(1, nodes, direct, 0)

        def passed(k, carry):
            source = lax.rem(l * nodes + nodes + k, devices)
            arrival(q, source).wait()
            return carry

        lax.fori_loop(0, devices - nodes, passed, 0)

    def unpack(q):
        for g in range(devices // group):
            landed = recv[q, g * group:(g + 1) * group].reshape(group * SLAB, WIDTH)
            chosen = dot(picks[...], landed)
            rows = group * CAP
            here = slice(g * rows, (g + 1) * rows)
            for c, block in enumerate(plan[q]):
                if block is None:
                    gate[here, :] = chosen[c * rows:(c + 1) * rows]
            for c, block in enumerate(plan[q]):
                if block is not None:
                    part = chosen[c * rows:(c + 1) * rows]
                    columns = slice(block * WIDTH, (block + 1) * WIDTH)
                    x[here, columns] = part.astype(bf16)
                    scaled[here, columns] = (gate[here, :] * part).astype(bf16)

    def span(q):
        blocks = [b for b in plan[q] if b is not None]
        return blocks[0] * WIDTH, (blocks[-1] + 1) * WIDTH

    def multiply(q):
        first, last = span(q)
        part = dot(x[:, first:last], weight[:, first:last], ((1,), (1,)))
        unscaled[...] = part if q == 0 else unscaled[...] + part

    tall = min(256, units)

    def update(q):
        first, last = span(q)

        def tile(i, carry):
            rows = pl.ds(pl.multiple_of(lax.rem(i, units // tall) * tall, tall), tall)
            columns = pl.ds(pl.multiple_of(first + (i // (units // tall)) * WIDTH, WIDTH), WIDTH)
            grad = dot(hidden_t[rows, :], scaled[:, columns])
            second_new = (
                beta_second * second[rows, columns].astype(f32)
                + ((1.0 - beta_second) * grad) * grad
            )
            y = second_new * (1.0 / correct_second)
            root = y * lax.rsqrt(y)
            step = (learn_rate * grad) * pl.reciprocal(root + epsilon, approx=True)
            weight_new = weight[rows, columns].astype(f32) * (1.0 - learn_rate * decay_rate) - step
            second_out[rows, columns] = second_new.astype(bf16)
            weight_out[rows, columns] = weight_new.astype(bf16)
            return carry

        lax.fori_loop(0, (units // tall) * ((last - first) // WIDTH), tile, 0)

    pack(0)
    pl.semaphore_wait(barrier, devices - 1)
    push(0)
    for q in range(1, len(plan)):
        pack(q)
        push(q)
    for q in range(len(plan)):
        hand_on(q, me)

    picked_row, picked_col = iota((group * CAP, group * SLAB), 0), iota((group * CAP, group * SLAB), 1)
    wanted = (picked_row // CAP) * SLAB + picked_row % CAP
    for c in range(BLOCKS):
        picks[c * group * CAP:(c + 1) * group * CAP, :] = jnp.where(
            picked_col == wanted + CAP * c, 1.0, 0.0
        ).astype(bf16)
    loads[1].wait()
    hidden_t[...] = hidden[...].astype(f32).T.astype(bf16)
    loads[2].wait()
    loads[3].wait()

    for q in range(len(plan)):
        gather(q)
        unpack(q)
        multiply(q)
        if q < len(plan) - 1:
            update(q)

    raw = unscaled[...]
    for j in range(0, units, LANES):
        hidden_out[:, j:j + LANES] = (gate[:, :LANES] * raw[:, j:j + LANES]).astype(bf16)
    terms = raw * hidden[...].astype(f32)
    folded = terms[:, :LANES]
    for j in range(LANES, units, LANES):
        folded += terms[:, j:j + LANES]
    for s in range(0, slots, LANES):
        part = folded[s:s + LANES]
        if part.shape[0] < LANES:
            part = jnp.concatenate([part, jnp.zeros((LANES - part.shape[0], LANES), f32)], 0)
        score_send[s // LANES] = jnp.sum(part.T, 0, keepdims=True)

    def answer(k, carry):
        other = lax.rem(me + k, devices)
        pltpu.make_async_remote_copy(
            src_ref=score_send.at[(CAP * other) // LANES], dst_ref=score_recv.at[me],
            send_sem=score_send_sem, recv_sem=score_recv_sem,
            device_id=(lax.rem(other, nodes), other // nodes), device_id_type=MESH,
        ).start()
        return carry

    lax.fori_loop(1, devices, answer, 0)
    score_recv[me] = score_send[(CAP * me) // LANES]

    update(len(plan) - 1)

    others = score_recv.at[pl.ds(0, devices - 1)]
    pltpu.make_async_copy(others, others, score_recv_sem).wait()
    sums = score_recv[0:nodes].reshape(nodes, LANES)
    for k in range(1, members):
        sums += score_recv[k * nodes:(k + 1) * nodes].reshape(nodes, LANES)
    lane = iota((nodes, LANES), 1) - lax.rem(CAP * me, LANES)
    token_score = jnp.zeros((1, tokens), f32)
    for r in range(CAP):
        column = jnp.sum(jnp.where(lane == r, sums, 0.0), 1, keepdims=True)
        column = jnp.sum(jnp.where(onehot > 0, column, 0.0), 0, keepdims=True)
        token_score += jnp.where(rank == r, column, 0.0)
    score_out[...] = jnp.where(hit, token_score, 0.0)

    pltpu.make_async_copy(others, others, score_send_sem).wait()
    for q in range(len(plan)):
        sent = send.at[q, pl.ds(0, nodes - 1)]
        pltpu.make_async_copy(sent, sent, send_sem.at[q]).wait()
        if members > 1:
            for _ in range(1):
                given = recv.at[q, pl.ds(0, nodes * (members - 1))]
                pltpu.make_async_copy(given, given, pass_sem.at[q]).wait()


def on_device(nodes, members, grad_out, expert_ids, gate_weights, saved_hidden, down_weight, second_moment):
    tokens, features = grad_out.shape
    _, slots, units = saved_hidden.shape
    devices = nodes * members
    group = min(32, devices)
    blocks = [None] + list(range(features // WIDTH))
    plan = [blocks[i:i + BLOCKS] for i in range(0, len(blocks), BLOCKS)]
    chunks = len(plan)
    small = pl.BlockSpec(memory_space=pltpu.VMEM)
    large = pl.BlockSpec(memory_space=pl.ANY)
    scores, hidden_grad, new_weight, new_second = pl.pallas_call(
        functools.partial(kernel, nodes, members, plan),
        out_shape=(
            pltpu.VMEM((expert_ids.shape[1], tokens), f32),
            pltpu.VMEM((slots, units), bf16),
            pltpu.VMEM((units, features), bf16),
            pltpu.VMEM((units, features), bf16),
        ),
        in_specs=[small, small, large, large, large, large],
        out_specs=(small, small, small, small),
        scratch_shapes=[
            pltpu.VMEM((tokens, features), bf16),
            pltpu.VMEM((slots, units), bf16),
            pltpu.VMEM((units, features), bf16),
            pltpu.VMEM((units, features), bf16),
            pltpu.VMEM((units, slots), bf16),
            pltpu.VMEM((chunks, nodes, SLAB, WIDTH), bf16),
            pltpu.VMEM((chunks, devices, SLAB, WIDTH), bf16),
            pltpu.VMEM((BLOCKS * group * CAP, group * SLAB), bf16),
            pltpu.VMEM((slots, features), bf16),
            pltpu.VMEM((slots, features), bf16),
            pltpu.VMEM((slots, WIDTH), f32),
            pltpu.VMEM((slots, units), f32),
            pltpu.VMEM((-(-slots // LANES), 1, LANES), f32),
            pltpu.VMEM((devices, 1, LANES), f32),
            pltpu.SemaphoreType.DMA((4,)),
            pltpu.SemaphoreType.DMA((chunks,)),
            pltpu.SemaphoreType.DMA((chunks, devices)),
            pltpu.SemaphoreType.DMA((chunks,)),
            pltpu.SemaphoreType.DMA,
            pltpu.SemaphoreType.DMA,
        ],
        compiler_params=pltpu.CompilerParams(
            collective_id=0, has_side_effects=True, vmem_limit_bytes=48 * 1024 * 1024
        ),
        cost_estimate=pl.CostEstimate(
            flops=4 * slots * units * features, bytes_accessed=8 * units * features, transcendentals=0
        ),
    )(expert_ids.T, gate_weights.T, grad_out, saved_hidden[0], down_weight[0], second_moment[0])
    return scores.T, hidden_grad[None], new_weight[None], new_second[None]


def solution(mesh):
    return jax.shard_map(
        functools.partial(on_device, mesh.shape["node"], mesh.shape["local"]),
        mesh=mesh,
        in_specs=(
            P(("node", "local"), None),
            P(("node", "local"), None),
            P(("node", "local"), None),
            P("node", None, "local"),
            P("node", "local", None),
            P("node", "local", None),
        ),
        out_specs=(
            P(("node", "local"), None),
            P("node", None, "local"),
            P("node", "local", None),
            P("node", "local", None),
        ),
        check_vma=False,
    )
```

```python
import functools

import jax
import jax.numpy as jnp
from jax import lax
from jax.experimental import pallas as pl
from jax.experimental.pallas import tpu as pltpu
from jax.sharding import PartitionSpec as P

MESH = pl.DeviceIdType.MESH
EXPERTS_PER_HOST = 4
CAP = 2
WIDTH = 256
SLAB = 16
BLOCKS = SLAB // CAP
LANES = 128
LATE = 5

beta_second = 0.95
learn_rate = 0.002
decay_rate = 0.1
epsilon = 1e-08
correct_second = 0.994079470779666

f32 = jnp.float32
bf16 = jnp.bfloat16


def dot(a, b, dims=((1,), (0,))):
    return lax.dot_general(a, b, (dims, ((), ())), preferred_element_type=f32)


def iota(shape, axis):
    return lax.broadcasted_iota(jnp.int32, shape, axis)


def adamw(hidden_t, scaled, weight, second):
    grad = dot(hidden_t, scaled)
    second_new = beta_second * second.astype(f32) + ((1.0 - beta_second) * grad) * grad
    y = second_new * (1.0 / correct_second)
    root = y * lax.rsqrt(y)
    step = (learn_rate * grad) * pl.reciprocal(root + epsilon, approx=True)
    weight_new = weight.astype(f32) * (1.0 - learn_rate * decay_rate) - step
    return weight_new.astype(bf16), second_new.astype(bf16)


def kernel(
    nodes, members, plan, early,
    ids_hbm, gates_hbm, grad_hbm, hidden_hbm, weight_hbm, second_hbm,
    score_out, hidden_out, weight, second, hidden_t, scaled,
    ids_ref, gates_ref, grads, hidden, send, recv, picks, x, gate,
    unscaled, score_send, score_recv,
    load_sem, send_sem, recv_sem, pass_sem, score_send_sem, score_recv_sem,
):
    n, l = lax.axis_index("node"), lax.axis_index("local")
    devices = nodes * members
    me = l * nodes + n
    tokens = grads.shape[0]
    slots, units = hidden.shape
    group = min(32, devices)

    loads = [
        pltpu.make_async_copy(source, target, load_sem.at[i])
        for i, (source, target) in enumerate(
            (
                (ids_hbm, ids_ref), (gates_hbm, gates_ref), (grad_hbm, grads),
                (hidden_hbm, hidden), (weight_hbm, weight), (second_hbm, second),
            )
        )
    ]
    for load in loads[:3]:
        load.start()

    barrier = pltpu.get_barrier_semaphore()

    def greet(k, carry):
        other = lax.rem(me + k, devices)
        pl.semaphore_signal(
            barrier, inc=1, device_id=(lax.rem(other, nodes), other // nodes), device_id_type=MESH
        )
        return carry

    lax.fori_loop(1, devices, greet, 0)

    loads[0].wait()
    loads[1].wait()
    ids = ids_ref[...]
    hit = ids % EXPERTS_PER_HOST == 0
    hit_one = jnp.where(hit, 1, 0)
    present = jnp.max(hit_one, 0, keepdims=True)
    dest = jnp.sum(jnp.where(hit, ids // EXPERTS_PER_HOST, 0), 0, keepdims=True)
    dest = jnp.where(present > 0, dest, -1)
    onehot = jnp.where(iota((nodes, tokens), 0) == dest, 1.0, 0.0).astype(f32)
    before = jnp.where(iota((tokens, tokens), 0) < iota((tokens, tokens), 1), 1.0, 0.0)
    earlier = dot(onehot.astype(bf16), before.astype(bf16))
    rank = jnp.sum(onehot * earlier, 0, keepdims=True).astype(jnp.int32)
    key = jnp.where(present > 0, dest * SLAB + rank, -SLAB * CAP)
    matched = jnp.sum(jnp.where(hit, gates_ref[...], 0.0), 0, keepdims=True)
    matched = matched.astype(bf16).astype(f32)

    loads[2].wait()
    for load in loads[3:]:
        load.start()
    place = iota((nodes * SLAB, tokens), 0)

    def pack(q):
        total = None
        for c in range(0, len(plan[q]), 2):
            masks, rights = [], []
            for block in plan[q][c:c + 2]:
                mask = place == key + CAP * (c + len(masks))
                if block is None:
                    masks.append(jnp.where(mask, matched, 0.0).astype(bf16))
                    rights.append(jnp.ones((tokens, WIDTH), bf16))
                else:
                    masks.append(jnp.where(mask, 1.0, 0.0).astype(bf16))
                    rights.append(grads[:, block * WIDTH:(block + 1) * WIDTH])
            part = dot(jnp.concatenate(masks, 1), jnp.concatenate(rights, 0))
            total = part if total is None else total + part
        send[q] = total.astype(bf16).reshape(nodes, SLAB, WIDTH)

    def turn(i):
        return nodes // 2 + ((i + 1) // 2) * (1 - 2 * lax.rem(i, 2))

    def push(q):
        def one(i, carry):
            other = lax.rem(n + turn(i), nodes)
            pltpu.make_async_remote_copy(
                src_ref=send.at[q, other], dst_ref=recv.at[q, me],
                send_sem=send_sem.at[q], recv_sem=recv_sem.at[q, me],
                device_id=(other, l), device_id_type=MESH,
            ).start()
            return carry

        lax.fori_loop(0, nodes - 1, one, 0)
        recv[q, me] = send[q, n]

    def hand_on(q, source):
        for k in range(1, members):
            pltpu.make_async_remote_copy(
                src_ref=recv.at[q, source], dst_ref=recv.at[q, source],
                send_sem=pass_sem.at[q], recv_sem=recv_sem.at[q, source],
                device_id=(n, lax.rem(l + k, members)), device_id_type=MESH,
            ).start()

    def arrival(q, source):
        return pltpu.make_async_copy(
            recv.at[q, source], recv.at[q, source], recv_sem.at[q, source]
        )

    def relay(q, i):
        source = l * nodes + lax.rem(n + nodes - turn(i), nodes)
        arrival(q, source).wait()
        hand_on(q, source)

    def relay_rest(q, first):
        def direct(i, carry):
            relay(q, i)
            return carry

        lax.fori_loop(first, nodes - 1, direct, 0)

    def collect(q):
        def passed(k, carry):
            arrival(q, lax.rem(l * nodes + nodes + k, devices)).wait()
            return carry

        lax.fori_loop(0, devices - nodes, passed, 0)

    def unpack(q):
        for g in range(devices // group):
            landed = recv[q, g * group:(g + 1) * group].reshape(group * SLAB, WIDTH)
            chosen = dot(picks[...], landed)
            rows = group * CAP
            here = slice(g * rows, (g + 1) * rows)
            for c, block in enumerate(plan[q]):
                if block is None:
                    gate[here, :] = chosen[c * rows:(c + 1) * rows]
            for c, block in enumerate(plan[q]):
                if block is not None:
                    part = chosen[c * rows:(c + 1) * rows]
                    columns = slice(block * WIDTH, (block + 1) * WIDTH)
                    x[here, columns] = part.astype(bf16)
                    scaled[here, columns] = (gate[here, :] * part).astype(bf16)

    def span(q):
        blocks = [b for b in plan[q] if b is not None]
        return blocks[0] * WIDTH, (blocks[-1] + 1) * WIDTH

    def multiply(q):
        first, last = span(q)
        part = dot(x[:, first:last], weight[:, first:last], ((1,), (1,)))
        unscaled[...] = part if q == 0 else unscaled[...] + part

    def update(first, last, relayed=None):
        tiles = (last - first) // WIDTH
        share = 0 if relayed is None else -(-(nodes - 1) // tiles)
        if share > 2:
            share = 2

        def tile(i, carry):
            columns = pl.ds(pl.multiple_of(first + i * WIDTH, WIDTH), WIDTH)
            weight[:, columns], second[:, columns] = adamw(
                hidden_t[...], scaled[:, columns], weight[:, columns], second[:, columns]
            )
            for j in range(share):
                @pl.when(i * share + j < nodes - 1)
                def _():
                    relay(relayed, i * share + j)
            return carry

        lax.fori_loop(0, tiles, tile, 0)
        if relayed is not None:
            relay_rest(relayed, min(share * tiles, nodes - 1))

    pack(0)
    pl.semaphore_wait(barrier, devices - 1)
    push(0)
    for q in range(1, len(plan)):
        pack(q)
        push(q)
    for q in range(len(plan)):
        hand_on(q, me)

    picked_row, picked_col = iota((group * CAP, group * SLAB), 0), iota((group * CAP, group * SLAB), 1)
    wanted = (picked_row // CAP) * SLAB + picked_row % CAP
    for c in range(BLOCKS):
        picks[c * group * CAP:(c + 1) * group * CAP, :] = jnp.where(
            picked_col == wanted + CAP * c, 1.0, 0.0
        ).astype(bf16)
    loads[3].wait()
    hidden_t[...] = hidden[...].astype(f32).T.astype(bf16)
    loads[4].wait()
    loads[5].wait()

    relay_rest(0, 0)
    for q in range(len(plan)):
        collect(q)
        unpack(q)
        multiply(q)
        if q < len(plan) - 1:
            update(*span(q), relayed=q + 1)

    raw = unscaled[...]
    for j in range(0, units, LANES):
        hidden_out[:, j:j + LANES] = (gate[:, :LANES] * raw[:, j:j + LANES]).astype(bf16)
    terms = raw * hidden[...].astype(f32)
    folded = terms[:, :LANES]
    for j in range(LANES, units, LANES):
        folded += terms[:, j:j + LANES]
    for s in range(0, slots, LANES):
        part = folded[s:s + LANES]
        if part.shape[0] < LANES:
            part = jnp.concatenate([part, jnp.zeros((LANES - part.shape[0], LANES), f32)], 0)
        score_send[s // LANES] = jnp.sum(part.T, 0, keepdims=True)

    def answer(k, carry):
        other = lax.rem(me + k, devices)
        pltpu.make_async_remote_copy(
            src_ref=score_send.at[(CAP * other) // LANES], dst_ref=score_recv.at[me],
            send_sem=score_send_sem, recv_sem=score_recv_sem,
            device_id=(lax.rem(other, nodes), other // nodes), device_id_type=MESH,
        ).start()
        return carry

    lax.fori_loop(1, devices, answer, 0)
    score_recv[me] = score_send[(CAP * me) // LANES]

    update(span(len(plan) - 1)[0], early)

    others = score_recv.at[pl.ds(0, devices - 1)]
    pltpu.make_async_copy(others, others, score_recv_sem).wait()
    sums = score_recv[0:nodes].reshape(nodes, LANES)
    for k in range(1, members):
        sums += score_recv[k * nodes:(k + 1) * nodes].reshape(nodes, LANES)
    lane = iota((nodes, LANES), 1) - lax.rem(CAP * me, LANES)
    token_score = jnp.zeros((1, tokens), f32)
    for r in range(CAP):
        column = jnp.sum(jnp.where(lane == r, sums, 0.0), 1, keepdims=True)
        column = jnp.sum(jnp.where(onehot > 0, column, 0.0), 0, keepdims=True)
        token_score += jnp.where(rank == r, column, 0.0)
    score_out[...] = jnp.where(hit, token_score, 0.0)

    pltpu.make_async_copy(others, others, score_send_sem).wait()
    for q in range(len(plan)):
        sent = send.at[q, pl.ds(0, nodes - 1)]
        pltpu.make_async_copy(sent, sent, send_sem.at[q]).wait()
        if members > 1:
            for _ in range(1):
                given = recv.at[q, pl.ds(0, nodes * (members - 1))]
                pltpu.make_async_copy(given, given, pass_sem.at[q]).wait()


def finish(
    early, scores, hidden_grad, weight, second, hidden_t, scaled,
    score_out, hidden_out, weight_out, second_out,
    weight_late, second_late, copy_sem,
):
    units, features = weight.shape
    copies = [
        pltpu.make_async_copy(scores, score_out, copy_sem.at[0]),
        pltpu.make_async_copy(hidden_grad, hidden_out, copy_sem.at[1]),
    ]
    pieces = 4
    for i in range(pieces):
        rows = pl.ds(i * (units // pieces), units // pieces)
        for j, (source, target) in enumerate(((weight, weight_out), (second, second_out))):
            copies.append(pltpu.make_async_copy(
                source.at[rows, pl.ds(0, early)], target.at[rows, pl.ds(0, early)],
                copy_sem.at[2 + 2 * i + j],
            ))
    for copy in copies:
        copy.start()
    base = 2 + 2 * pieces
    for i, first in enumerate(range(early, features, WIDTH)):
        columns, late = pl.ds(first, WIDTH), pl.ds(first - early, WIDTH)
        weight_late[:, late], second_late[:, late] = adamw(
            hidden_t[...], scaled[:, columns], weight[:, columns], second[:, columns]
        )
        for j, (source, target) in enumerate(((weight_late, weight_out), (second_late, second_out))):
            copies.append(pltpu.make_async_copy(
                source.at[:, late], target.at[:, columns], copy_sem.at[base + 2 * i + j]
            ))
            copies[-1].start()
    for copy in copies:
        copy.wait()


def on_device(nodes, members, grad_out, expert_ids, gate_weights, saved_hidden, down_weight, second_moment):
    tokens, features = grad_out.shape
    _, slots, units = saved_hidden.shape
    chosen = expert_ids.shape[1]
    devices = nodes * members
    group = min(32, devices)
    blocks = [None] + list(range(features // WIDTH))
    plan = [blocks[i:i + BLOCKS] for i in range(0, len(blocks), BLOCKS)]
    chunks = len(plan)
    early = features - LATE * WIDTH
    small = pl.BlockSpec(memory_space=pltpu.VMEM)
    large = pl.BlockSpec(memory_space=pl.ANY)
    kept = pl.pallas_call(
        functools.partial(kernel, nodes, members, plan, early),
        out_shape=(
            pltpu.VMEM((chosen, tokens), f32),
            pltpu.VMEM((slots, units), bf16),
            pltpu.VMEM((units, features), bf16),
            pltpu.VMEM((units, features), bf16),
            pltpu.VMEM((units, slots), bf16),
            pltpu.VMEM((slots, features), bf16),
        ),
        in_specs=[large] * 6,
        out_specs=(small,) * 6,
        scratch_shapes=[
            pltpu.VMEM((chosen, tokens), jnp.int32),
            pltpu.VMEM((chosen, tokens), f32),
            pltpu.VMEM((tokens, features), bf16),
            pltpu.VMEM((slots, units), bf16),
            pltpu.VMEM((chunks, nodes, SLAB, WIDTH), bf16),
            pltpu.VMEM((chunks, devices, SLAB, WIDTH), bf16),
            pltpu.VMEM((BLOCKS * group * CAP, group * SLAB), bf16),
            pltpu.VMEM((slots, features), bf16),
            pltpu.VMEM((slots, WIDTH), f32),
            pltpu.VMEM((slots, units), f32),
            pltpu.VMEM((-(-slots // LANES), 1, LANES), f32),
            pltpu.VMEM((devices, 1, LANES), f32),
            pltpu.SemaphoreType.DMA((6,)),
            pltpu.SemaphoreType.DMA((chunks,)),
            pltpu.SemaphoreType.DMA((chunks, devices)),
            pltpu.SemaphoreType.DMA((chunks,)),
            pltpu.SemaphoreType.DMA,
            pltpu.SemaphoreType.DMA,
        ],
        compiler_params=pltpu.CompilerParams(
            collective_id=0, has_side_effects=True, vmem_limit_bytes=48 * 1024 * 1024
        ),
        cost_estimate=pl.CostEstimate(
            flops=4 * slots * units * features, bytes_accessed=4 * units * features, transcendentals=0
        ),
    )(expert_ids.T, gate_weights.T, grad_out, saved_hidden[0], down_weight[0], second_moment[0])
    kept = [pltpu.with_memory_space_constraint(a, pltpu.VMEM) for a in kept]
    scores, hidden_grad, new_weight, new_second = pl.pallas_call(
        functools.partial(finish, early),
        out_shape=(
            jax.ShapeDtypeStruct((chosen, tokens), f32),
            jax.ShapeDtypeStruct((slots, units), bf16),
            jax.ShapeDtypeStruct((units, features), bf16),
            jax.ShapeDtypeStruct((units, features), bf16),
        ),
        in_specs=[small] * 6,
        out_specs=(large,) * 4,
        scratch_shapes=[
            pltpu.VMEM((units, features - early), bf16),
            pltpu.VMEM((units, features - early), bf16),
            pltpu.SemaphoreType.DMA((10 + 2 * LATE,)),
        ],
        compiler_params=pltpu.CompilerParams(vmem_limit_bytes=24 * 1024 * 1024),
        cost_estimate=pl.CostEstimate(
            flops=2 * slots * units * LATE * WIDTH, bytes_accessed=4 * units * features, transcendentals=0
        ),
    )(*kept)
    return scores.T, hidden_grad[None], new_weight[None], new_second[None]


def solution(mesh):
    return jax.shard_map(
        functools.partial(on_device, mesh.shape["node"], mesh.shape["local"]),
        mesh=mesh,
        in_specs=(
            P(("node", "local"), None),
            P(("node", "local"), None),
            P(("node", "local"), None),
            P("node", None, "local"),
            P("node", "local", None),
            P("node", "local", None),
        ),
        out_specs=(
            P(("node", "local"), None),
            P("node", None, "local"),
            P("node", "local", None),
            P("node", "local", None),
        ),
        check_vma=False,
    )
```

```python
import functools

import jax
import jax.numpy as jnp
from jax import lax
from jax.experimental import pallas as pl
from jax.experimental.pallas import tpu as pltpu
from jax.sharding import PartitionSpec as P

MESH = pl.DeviceIdType.MESH
EXPERTS_PER_HOST = 4
CAP = 2
WIDTH = 256
SLAB = 16
BLOCKS = SLAB // CAP
LANES = 128
LATE = 6

beta_second = 0.95
learn_rate = 0.002
decay_rate = 0.1
epsilon = 1e-08
correct_second = 0.994079470779666

f32 = jnp.float32
bf16 = jnp.bfloat16


def dot(a, b, dims=((1,), (0,))):
    return lax.dot_general(a, b, (dims, ((), ())), preferred_element_type=f32)


def iota(shape, axis):
    return lax.broadcasted_iota(jnp.int32, shape, axis)


def adamw(hidden_t, scaled, weight, second):
    grad = dot(hidden_t, scaled)
    second_new = second + ((1.0 - beta_second) * grad) * grad
    root = second_new * lax.rsqrt(second_new) + epsilon * correct_second ** 0.5
    step = (learn_rate * correct_second ** 0.5 * grad) * pl.reciprocal(root, approx=True)
    return (weight - step).astype(bf16), second_new.astype(bf16)


def kernel(
    nodes, members, plan, early,
    ids_hbm, gates_hbm, grad_hbm, hidden_hbm, weight_hbm, second_hbm,
    score_out, hidden_out, weight_out, second_out, weight_decayed, second_decayed, hidden_t, scaled,
    ids_ref, gates_ref, grads, hidden, weight, second, send, recv, picks, x, gate,
    unscaled, score_send, score_parts, score_recv,
    load_sem, send_sem, recv_sem, pass_send_sem, pass_recv_sem,
    part_send_sem, part_recv_sem, score_send_sem, score_recv_sem,
):
    n, l = lax.axis_index("node"), lax.axis_index("local")
    devices = nodes * members
    me = l * nodes + n
    tokens = grads.shape[0]
    slots, units = hidden.shape
    group = min(32, devices)

    loads = [
        pltpu.make_async_copy(source, target, load_sem.at[i])
        for i, (source, target) in enumerate(
            (
                (ids_hbm, ids_ref), (gates_hbm, gates_ref), (grad_hbm, grads),
                (hidden_hbm, hidden), (weight_hbm, weight), (second_hbm, second),
            )
        )
    ]
    for load in loads[:3]:
        load.start()

    barrier = pltpu.get_barrier_semaphore()

    def greet(k, carry):
        pl.semaphore_signal(
            barrier, inc=1, device_id=(lax.rem(n + k, nodes), l), device_id_type=MESH
        )
        return carry

    lax.fori_loop(1, nodes, greet, 0)
    siblings = [(n, lax.rem(l + k, members)) for k in range(1, members)]
    for sibling in siblings:
        pl.semaphore_signal(barrier, inc=1, device_id=sibling, device_id_type=MESH)

    loads[0].wait()
    loads[1].wait()
    ids = ids_ref[...]
    hit = ids % EXPERTS_PER_HOST == 0
    hit_one = jnp.where(hit, 1, 0)
    present = jnp.max(hit_one, 0, keepdims=True)
    dest = jnp.sum(jnp.where(hit, ids // EXPERTS_PER_HOST, 0), 0, keepdims=True)
    dest = jnp.where(present > 0, dest, -1)
    onehot = jnp.where(iota((nodes, tokens), 0) == dest, 1.0, 0.0).astype(f32)
    before = jnp.where(iota((tokens, tokens), 0) < iota((tokens, tokens), 1), 1.0, 0.0)
    earlier = dot(onehot.astype(bf16), before.astype(bf16))
    rank = jnp.sum(onehot * earlier, 0, keepdims=True).astype(jnp.int32)
    key = jnp.where(present > 0, dest * SLAB + rank, -SLAB * CAP)
    matched = jnp.sum(jnp.where(hit, gates_ref[...], 0.0), 0, keepdims=True)
    matched = matched.astype(bf16).astype(f32)

    loads[2].wait()
    for load in loads[3:]:
        load.start()
    place = iota((nodes * SLAB, tokens), 0)

    def pack(q):
        total = None
        for c in range(0, len(plan[q]), 2):
            masks, rights = [], []
            for block in plan[q][c:c + 2]:
                mask = place == key + CAP * (c + len(masks))
                if block is None:
                    masks.append(jnp.where(mask, matched, 0.0).astype(bf16))
                    rights.append(jnp.ones((tokens, WIDTH), bf16))
                else:
                    masks.append(jnp.where(mask, 1.0, 0.0).astype(bf16))
                    rights.append(grads[:, block * WIDTH:(block + 1) * WIDTH])
            part = dot(jnp.concatenate(masks, 1), jnp.concatenate(rights, 0))
            total = part if total is None else total + part
        send[q] = total.astype(bf16).reshape(nodes, SLAB, WIDTH)

    def turn(i):
        return nodes // 2 + ((i + 1) // 2) * (1 - 2 * lax.rem(i, 2))

    def push(q):
        def one(i, carry):
            other = lax.rem(n + turn(i), nodes)
            pltpu.make_async_remote_copy(
                src_ref=send.at[q, other], dst_ref=recv.at[q, me],
                send_sem=send_sem.at[q], recv_sem=recv_sem.at[q],
                device_id=(other, l), device_id_type=MESH,
            ).start()
            return carry

        lax.fori_loop(0, nodes - 1, one, 0)
        recv[q, me] = send[q, n]

    def settle(ref, sem):
        pltpu.make_async_copy(ref, ref, sem).wait()

    def relay(q):
        settle(recv.at[q, pl.ds(0, nodes - 1)], recv_sem.at[q])
        mine = recv.at[q, pl.ds(l * nodes, nodes)]
        for sibling in siblings:
            pltpu.make_async_remote_copy(
                src_ref=mine, dst_ref=mine,
                send_sem=pass_send_sem.at[q], recv_sem=pass_recv_sem.at[q],
                device_id=sibling, device_id_type=MESH,
            ).start()

    def collect(q):
        settle(recv.at[q, pl.ds(0, devices - nodes)], pass_recv_sem.at[q])

    def unpack(q):
        for g in range(devices // group):
            landed = recv[q, g * group:(g + 1) * group].reshape(group * SLAB, WIDTH)
            chosen = dot(picks[...], landed)
            rows = group * CAP
            here = slice(g * rows, (g + 1) * rows)
            for c, block in enumerate(plan[q]):
                if block is None:
                    gate[here, :] = chosen[c * rows:(c + 1) * rows]
            for c, block in enumerate(plan[q]):
                if block is not None:
                    part = chosen[c * rows:(c + 1) * rows]
                    columns = slice(block * WIDTH, (block + 1) * WIDTH)
                    x[here, columns] = part.astype(bf16)
                    scaled[here, columns] = (gate[here, :] * part).astype(bf16)

    def span(q):
        blocks = [b for b in plan[q] if b is not None]
        return blocks[0] * WIDTH, (blocks[-1] + 1) * WIDTH

    def multiply(q):
        first, last = span(q)
        part = dot(x[:, first:last], weight[:, first:last], ((1,), (1,)))
        unscaled[...] = part if q == 0 else unscaled[...] + part

    def decay():
        def tile(i, carry):
            columns = pl.ds(pl.multiple_of(i * WIDTH, WIDTH), WIDTH)
            weight_decayed[:, columns] = weight[:, columns].astype(f32) * (1.0 - learn_rate * decay_rate)
            second_decayed[:, columns] = second[:, columns].astype(f32) * beta_second
            return carry

        lax.fori_loop(0, weight.shape[1] // WIDTH, tile, 0)

    def update(first, last):
        def tile(i, carry):
            columns = pl.ds(pl.multiple_of(i * WIDTH, WIDTH), WIDTH)
            weight_out[:, columns], second_out[:, columns] = adamw(
                hidden_t[...], scaled[:, columns], weight_decayed[:, columns], second_decayed[:, columns]
            )
            return carry

        lax.fori_loop(first, last, tile, 0)

    pack(0)
    pl.semaphore_wait(barrier, nodes - 1 + members - 1)
    push(0)
    for q in range(1, len(plan)):
        pack(q)
        push(q)
    picked_row, picked_col = iota((group * CAP, group * SLAB), 0), iota((group * CAP, group * SLAB), 1)
    wanted = (picked_row // CAP) * SLAB + picked_row % CAP
    for c in range(BLOCKS):
        picks[c * group * CAP:(c + 1) * group * CAP, :] = jnp.where(
            picked_col == wanted + CAP * c, 1.0, 0.0
        ).astype(bf16)
    loads[3].wait()
    hidden_t[...] = hidden[...].astype(f32).T.astype(bf16)
    loads[4].wait()
    loads[5].wait()

    decay()

    relay(0)
    for q in range(len(plan)):
        collect(q)
        unpack(q)
        multiply(q)
        if q < len(plan) - 1:
            relay(q + 1)
            update(early[q], early[q + 1])

    raw = unscaled[...]
    for j in range(0, units, LANES):
        hidden_out[:, j:j + LANES] = (gate[:, :LANES] * raw[:, j:j + LANES]).astype(bf16)
    terms = raw * hidden[...].astype(f32)
    folded = terms[:, :LANES]
    for j in range(LANES, units, LANES):
        folded += terms[:, j:j + LANES]
    for s in range(0, slots, LANES):
        part = folded[s:s + LANES]
        if part.shape[0] < LANES:
            part = jnp.concatenate([part, jnp.zeros((LANES - part.shape[0], LANES), f32)], 0)
        score_send[s // LANES] = jnp.sum(part.T, 0, keepdims=True)

    score_parts[l] = jnp.zeros_like(score_send)
    for sibling in siblings:
        pltpu.make_async_remote_copy(
            src_ref=score_send, dst_ref=score_parts.at[l],
            send_sem=part_send_sem, recv_sem=part_recv_sem,
            device_id=sibling, device_id_type=MESH,
        ).start()
    update(early[-3], early[-2])
    settle(score_parts.at[pl.ds(0, members - 1)], part_recv_sem)
    settle(score_parts.at[pl.ds(0, members - 1)], part_send_sem)
    for k in range(members):
        score_send[...] += score_parts[k]

    def answer(k, carry):
        other = lax.rem(n + k, nodes)
        pltpu.make_async_remote_copy(
            src_ref=score_send.at[(CAP * (l * nodes + other)) // LANES], dst_ref=score_recv.at[n],
            send_sem=score_send_sem, recv_sem=score_recv_sem,
            device_id=(other, l), device_id_type=MESH,
        ).start()
        return carry

    lax.fori_loop(1, nodes, answer, 0)
    score_recv[n] = score_send[(CAP * me) // LANES]
    update(early[-2], early[-1])

    others = score_recv.at[pl.ds(0, nodes - 1)]
    settle(others, score_recv_sem)
    sums = score_recv[...].reshape(nodes, LANES)
    lane = iota((nodes, LANES), 1) - lax.rem(CAP * me, LANES)
    token_score = jnp.zeros((1, tokens), f32)
    for r in range(CAP):
        column = jnp.sum(jnp.where(lane == r, sums, 0.0), 1, keepdims=True)
        column = jnp.sum(jnp.where(onehot > 0, column, 0.0), 0, keepdims=True)
        token_score += jnp.where(rank == r, column, 0.0)
    score_out[...] = jnp.where(hit, token_score, 0.0)

    settle(others, score_send_sem)
    for q in range(len(plan)):
        settle(send.at[q, pl.ds(0, nodes - 1)], send_sem.at[q])
        settle(recv.at[q, pl.ds(0, devices - nodes)], pass_send_sem.at[q])


def finish(
    early, scores, hidden_grad, weight, second, weight_decayed, second_decayed, hidden_t, scaled,
    score_out, hidden_out, weight_out, second_out,
    weight_late, second_late, copy_sem,
):
    units, features = weight.shape
    copies = [
        pltpu.make_async_copy(scores, score_out, copy_sem.at[0]),
        pltpu.make_async_copy(hidden_grad, hidden_out, copy_sem.at[1]),
    ]
    pieces = 4
    for i in range(pieces):
        rows = pl.ds(i * (units // pieces), units // pieces)
        for j, (source, target) in enumerate(((weight, weight_out), (second, second_out))):
            copies.append(pltpu.make_async_copy(
                source.at[rows, pl.ds(0, early)], target.at[rows, pl.ds(0, early)],
                copy_sem.at[2 + 2 * i + j],
            ))
    for copy in copies:
        copy.start()
    base = 2 + 2 * pieces
    for i, first in enumerate(range(early, features, WIDTH)):
        columns, late = pl.ds(first, WIDTH), pl.ds(first - early, WIDTH)
        weight_late[:, late], second_late[:, late] = adamw(
            hidden_t[...], scaled[:, columns], weight_decayed[:, columns], second_decayed[:, columns]
        )
        for j, (source, target) in enumerate(((weight_late, weight_out), (second_late, second_out))):
            copies.append(pltpu.make_async_copy(
                source.at[:, late], target.at[:, columns], copy_sem.at[base + 2 * i + j]
            ))
            copies[-1].start()
    for copy in copies:
        copy.wait()


def on_device(nodes, members, grad_out, expert_ids, gate_weights, saved_hidden, down_weight, second_moment):
    tokens, features = grad_out.shape
    _, slots, units = saved_hidden.shape
    chosen = expert_ids.shape[1]
    devices = nodes * members
    group = min(32, devices)
    blocks = [None] + list(range(features // WIDTH))
    plan = [blocks[i:i + BLOCKS] for i in range(0, len(blocks), BLOCKS)]
    chunks = len(plan)
    ahead = features // WIDTH - LATE
    gaps = [0, (3 * ahead) // 8, (5 * ahead) // 8, ahead]
    early = ahead * WIDTH
    small = pl.BlockSpec(memory_space=pltpu.VMEM)
    large = pl.BlockSpec(memory_space=pl.ANY)
    kept = pl.pallas_call(
        functools.partial(kernel, nodes, members, plan, gaps),
        out_shape=(
            pltpu.VMEM((chosen, tokens), f32),
            pltpu.VMEM((slots, units), bf16),
            pltpu.VMEM((units, features), bf16),
            pltpu.VMEM((units, features), bf16),
            pltpu.VMEM((units, features), f32),
            pltpu.VMEM((units, features), f32),
            pltpu.VMEM((units, slots), bf16),
            pltpu.VMEM((slots, features), bf16),
        ),
        in_specs=[large] * 6,
        out_specs=(small,) * 8,
        scratch_shapes=[
            pltpu.VMEM((chosen, tokens), jnp.int32),
            pltpu.VMEM((chosen, tokens), f32),
            pltpu.VMEM((tokens, features), bf16),
            pltpu.VMEM((slots, units), bf16),
            pltpu.VMEM((units, features), bf16),
            pltpu.VMEM((units, features), bf16),
            pltpu.VMEM((chunks, nodes, SLAB, WIDTH), bf16),
            pltpu.VMEM((chunks, devices, SLAB, WIDTH), bf16),
            pltpu.VMEM((BLOCKS * group * CAP, group * SLAB), bf16),
            pltpu.VMEM((slots, features), bf16),
            pltpu.VMEM((slots, WIDTH), f32),
            pltpu.VMEM((slots, units), f32),
            pltpu.VMEM((-(-slots // LANES), 1, LANES), f32),
            pltpu.VMEM((members, -(-slots // LANES), 1, LANES), f32),
            pltpu.VMEM((nodes, 1, LANES), f32),
            pltpu.SemaphoreType.DMA((6,)),
            pltpu.SemaphoreType.DMA((chunks,)),
            pltpu.SemaphoreType.DMA((chunks,)),
            pltpu.SemaphoreType.DMA((chunks,)),
            pltpu.SemaphoreType.DMA((chunks,)),
            pltpu.SemaphoreType.DMA,
            pltpu.SemaphoreType.DMA,
            pltpu.SemaphoreType.DMA,
            pltpu.SemaphoreType.DMA,
        ],
        compiler_params=pltpu.CompilerParams(
            collective_id=0, has_side_effects=True, vmem_limit_bytes=36 * 1024 * 1024
        ),
        cost_estimate=pl.CostEstimate(
            flops=4 * slots * units * features, bytes_accessed=4 * units * features, transcendentals=0
        ),
    )(expert_ids.T, gate_weights.T, grad_out, saved_hidden[0], down_weight[0], second_moment[0])
    kept = [pltpu.with_memory_space_constraint(a, pltpu.VMEM) for a in kept]
    scores, hidden_grad, new_weight, new_second = pl.pallas_call(
        functools.partial(finish, early),
        out_shape=(
            jax.ShapeDtypeStruct((chosen, tokens), f32),
            jax.ShapeDtypeStruct((slots, units), bf16),
            jax.ShapeDtypeStruct((units, features), bf16),
            jax.ShapeDtypeStruct((units, features), bf16),
        ),
        in_specs=[small] * 8,
        out_specs=(large,) * 4,
        scratch_shapes=[
            pltpu.VMEM((units, features - early), bf16),
            pltpu.VMEM((units, features - early), bf16),
            pltpu.SemaphoreType.DMA((10 + 2 * LATE,)),
        ],
        compiler_params=pltpu.CompilerParams(vmem_limit_bytes=16 * 1024 * 1024),
        cost_estimate=pl.CostEstimate(
            flops=2 * slots * units * LATE * WIDTH, bytes_accessed=4 * units * features, transcendentals=0
        ),
    )(*kept)
    return scores.T, hidden_grad[None], new_weight[None], new_second[None]


def solution(mesh):
    return jax.shard_map(
        functools.partial(on_device, mesh.shape["node"], mesh.shape["local"]),
        mesh=mesh,
        in_specs=(
            P(("node", "local"), None),
            P(("node", "local"), None),
            P(("node", "local"), None),
            P("node", None, "local"),
            P("node", "local", None),
            P("node", "local", None),
        ),
        out_specs=(
            P(("node", "local"), None),
            P("node", None, "local"),
            P("node", "local", None),
            P("node", "local", None),
        ),
        check_vma=False,
    )
```

```python
import functools

import jax
import jax.numpy as jnp
from jax import lax
from jax.experimental import pallas as pl
from jax.experimental.pallas import tpu as pltpu
from jax.sharding import PartitionSpec as P

MESH = pl.DeviceIdType.MESH
EXPERTS_PER_HOST = 4
CAP = 2
WIDTH = 256
SLAB = 16
BLOCKS = SLAB // CAP
LANES = 128
LATE = 7

beta_second = 0.95
learn_rate = 0.002
decay_rate = 0.1
epsilon = 1e-08
correct_second = 0.994079470779666

f32 = jnp.float32
bf16 = jnp.bfloat16


def dot(a, b, dims=((1,), (0,))):
    return lax.dot_general(a, b, (dims, ((), ())), preferred_element_type=f32)


def iota(shape, axis):
    return lax.broadcasted_iota(jnp.int32, shape, axis)


def adamw(hidden_t, scaled, weight, second):
    grad = dot(hidden_t, scaled)
    second_new = second + ((1.0 - beta_second) * grad) * grad
    root = second_new * lax.rsqrt(second_new) + epsilon * correct_second ** 0.5
    step = (learn_rate * correct_second ** 0.5 * grad) * pl.reciprocal(root, approx=True)
    return (weight - step).astype(bf16), second_new.astype(bf16)


def kernel(
    nodes, members, plan, early,
    ids_hbm, gates_hbm, grad_hbm, hidden_hbm, weight_hbm, second_hbm,
    score_out, hidden_out, weight_out, second_out, weight_decayed, second_decayed, hidden_t, scaled,
    ids_ref, gates_ref, grads, hidden, weight, second, send, recv, picks, x, gate,
    unscaled, back, back_parts, score_sums, score_send, score_recv,
    load_sem, send_sem, recv_sem, pass_send_sem, pass_recv_sem,
    back_send_sem, back_recv_sem, score_send_sem, score_recv_sem,
):
    n, l = lax.axis_index("node"), lax.axis_index("local")
    devices = nodes * members
    me = l * nodes + n
    tokens = grads.shape[0]
    slots, units = hidden.shape
    group = min(16, nodes)
    half = nodes * CAP

    loads = [
        pltpu.make_async_copy(source, target, load_sem.at[i])
        for i, (source, target) in enumerate(
            (
                (ids_hbm, ids_ref), (gates_hbm, gates_ref), (grad_hbm, grads),
                (hidden_hbm, hidden), (weight_hbm, weight), (second_hbm, second),
            )
        )
    ]
    for load in loads[:3]:
        load.start()

    barrier = pltpu.get_barrier_semaphore()

    def greet(k, carry):
        pl.semaphore_signal(
            barrier, inc=1, device_id=(lax.rem(n + k, nodes), l), device_id_type=MESH
        )
        return carry

    lax.fori_loop(1, nodes, greet, 0)
    siblings = [(n, lax.rem(l + k, members)) for k in range(1, members)]
    for sibling in siblings:
        pl.semaphore_signal(barrier, inc=1, device_id=sibling, device_id_type=MESH)

    loads[0].wait()
    loads[1].wait()
    ids = ids_ref[...]
    hit = ids % EXPERTS_PER_HOST == 0
    hit_one = jnp.where(hit, 1, 0)
    present = jnp.max(hit_one, 0, keepdims=True)
    dest = jnp.sum(jnp.where(hit, ids // EXPERTS_PER_HOST, 0), 0, keepdims=True)
    dest = jnp.where(present > 0, dest, -1)
    onehot = jnp.where(iota((nodes, tokens), 0) == dest, 1.0, 0.0).astype(f32)
    before = jnp.where(iota((tokens, tokens), 0) < iota((tokens, tokens), 1), 1.0, 0.0)
    earlier = dot(onehot.astype(bf16), before.astype(bf16))
    rank = jnp.sum(onehot * earlier, 0, keepdims=True).astype(jnp.int32)
    key = jnp.where(present > 0, dest * SLAB + rank, -SLAB * CAP)
    matched = jnp.sum(jnp.where(hit, gates_ref[...], 0.0), 0, keepdims=True)
    matched = matched.astype(bf16).astype(f32)

    loads[2].wait()
    for load in loads[3:]:
        load.start()
    place = iota((nodes * SLAB, tokens), 0)

    def pack(q):
        total = None
        for c in range(0, len(plan[q]), 2):
            masks, rights = [], []
            for block in plan[q][c:c + 2]:
                mask = place == key + CAP * (c + len(masks))
                if block is None:
                    masks.append(jnp.where(mask, matched, 0.0).astype(bf16))
                    rights.append(jnp.ones((tokens, WIDTH), bf16))
                else:
                    masks.append(jnp.where(mask, 1.0, 0.0).astype(bf16))
                    rights.append(grads[:, block * WIDTH:(block + 1) * WIDTH])
            part = dot(jnp.concatenate(masks, 1), jnp.concatenate(rights, 0))
            total = part if total is None else total + part
        send[q] = total.astype(bf16).reshape(nodes, SLAB, WIDTH)

    def turn(i):
        return nodes // 2 + ((i + 1) // 2) * (1 - 2 * lax.rem(i, 2))

    def push(q):
        def one(i, carry):
            other = lax.rem(n + turn(i), nodes)
            pltpu.make_async_remote_copy(
                src_ref=send.at[q, other], dst_ref=recv.at[q, me],
                send_sem=send_sem.at[q], recv_sem=recv_sem.at[q],
                device_id=(other, l), device_id_type=MESH,
            ).start()
            return carry

        lax.fori_loop(0, nodes - 1, one, 0)
        recv[q, me] = send[q, n]

    def settle(ref, sem):
        pltpu.make_async_copy(ref, ref, sem).wait()

    def relay(q):
        settle(recv.at[q, pl.ds(0, nodes - 1)], recv_sem.at[q])
        mine = recv.at[q, pl.ds(l * nodes, nodes)]
        for sibling in siblings:
            pltpu.make_async_remote_copy(
                src_ref=mine, dst_ref=mine,
                send_sem=pass_send_sem.at[q], recv_sem=pass_recv_sem.at[q],
                device_id=sibling, device_id_type=MESH,
            ).start()

    def collect(q):
        settle(recv.at[q, pl.ds(0, devices - nodes)], pass_recv_sem.at[q])

    def unpack(q, member, scored=False):
        rows = group * CAP
        for g in range(nodes // group):
            source = member * nodes + g * group
            landed = recv[q, pl.ds(source, group)].reshape(group * SLAB, WIDTH)
            chosen = dot(picks[...], landed)
            here = pl.ds(pl.multiple_of(source * CAP, rows), rows)
            local = slice(g * rows, (g + 1) * rows)
            if None in plan[q]:
                c = plan[q].index(None)
                gate[here, :] = chosen[c * rows:(c + 1) * rows]
            factor = gate[here, :]
            sums = None
            for c, block in enumerate(plan[q]):
                if block is None:
                    continue
                part = chosen[c * rows:(c + 1) * rows]
                columns = slice(block * WIDTH, (block + 1) * WIDTH)
                x[here, columns] = part.astype(bf16)
                scaled[here, columns] = (factor * part).astype(bf16)
                if scored:
                    against = back[here, columns].astype(f32)
                    for k in range(members - 1):
                        against += back_parts[k, local, columns].astype(f32)
                    term = part * against
                    sums = term if sums is None else sums + term
            if scored:
                sums = sums[:, :LANES] + sums[:, LANES:]
                score_sums[local, :] = sums if q == 0 else score_sums[local, :] + sums

    def span(q):
        blocks = [b for b in plan[q] if b is not None]
        return blocks[0] * WIDTH, (blocks[-1] + 1) * WIDTH

    def multiply(q):
        first, last = span(q)
        part = dot(x[:, first:last], weight[:, first:last], ((1,), (1,)))
        unscaled[...] = part if q == 0 else unscaled[...] + part

    def decay():
        def tile(i, carry):
            columns = pl.ds(pl.multiple_of(i * WIDTH, WIDTH), WIDTH)
            weight_decayed[:, columns] = weight[:, columns].astype(f32) * (1.0 - learn_rate * decay_rate)
            second_decayed[:, columns] = second[:, columns].astype(f32) * beta_second
            return carry

        lax.fori_loop(0, weight.shape[1] // WIDTH, tile, 0)

    def update(first, last):
        def tile(i, carry):
            columns = pl.ds(pl.multiple_of(i * WIDTH, WIDTH), WIDTH)
            weight_out[:, columns], second_out[:, columns] = adamw(
                hidden_t[...], scaled[:, columns], weight_decayed[:, columns], second_decayed[:, columns]
            )
            return carry

        lax.fori_loop(first, last, tile, 0)

    pack(0)
    pl.semaphore_wait(barrier, nodes - 1 + members - 1)
    push(0)
    for q in range(1, len(plan)):
        pack(q)
        push(q)
    loads[3].wait()
    loads[4].wait()
    features = weight.shape[1]
    stripe = 2 * WIDTH
    for j in range(0, features, stripe):
        back[:, j:j + stripe] = dot(hidden[...], weight[:, j:j + stripe]).astype(back.dtype)
    for k in range(1, members):
        other = lax.rem(l + k, members)
        pltpu.make_async_remote_copy(
            src_ref=back.at[pl.ds(pl.multiple_of(other * half, half), half)], dst_ref=back_parts.at[k - 1],
            send_sem=back_send_sem.at[k - 1], recv_sem=back_recv_sem.at[k - 1],
            device_id=(n, other), device_id_type=MESH,
        ).start()

    picked_row, picked_col = iota((group * CAP, group * SLAB), 0), iota((group * CAP, group * SLAB), 1)
    wanted = (picked_row // CAP) * SLAB + picked_row % CAP
    for c in range(BLOCKS):
        picks[c * group * CAP:(c + 1) * group * CAP, :] = jnp.where(
            picked_col == wanted + CAP * c, 1.0, 0.0
        ).astype(bf16)
    hidden_t[...] = hidden[...].astype(f32).T.astype(bf16)
    loads[5].wait()

    decay()

    for k in range(members - 1):
        settle(back_parts.at[k], back_recv_sem.at[k])
    for q in range(len(plan)):
        relay(q)
        unpack(q, l, scored=True)
        if q == len(plan) - 1:
            for s in range(0, half, LANES):
                part = score_sums[s:min(s + LANES, half), :]
                if part.shape[0] < LANES:
                    part = jnp.concatenate([part, jnp.zeros((LANES - part.shape[0], LANES), f32)], 0)
                score_send[s // LANES] = jnp.sum(part.T, 0, keepdims=True)

            def answer(i, carry):
                other = lax.rem(n + turn(i), nodes)
                pltpu.make_async_remote_copy(
                    src_ref=score_send.at[(CAP * other) // LANES], dst_ref=score_recv.at[n],
                    send_sem=score_send_sem, recv_sem=score_recv_sem,
                    device_id=(other, l), device_id_type=MESH,
                ).start()
                return carry

            lax.fori_loop(0, nodes - 1, answer, 0)
            score_recv[n] = score_send[(CAP * n) // LANES]
        collect(q)
        for k in range(1, members):
            unpack(q, lax.rem(l + k, members))
        multiply(q)
        if q < len(plan) - 1:
            update(early[q], early[q + 1])

    raw = unscaled[...]
    for j in range(0, units, LANES):
        hidden_out[:, j:j + LANES] = (gate[:, :LANES] * raw[:, j:j + LANES]).astype(bf16)
    update(early[-2], early[-1])

    others = score_recv.at[pl.ds(0, nodes - 1)]
    settle(others, score_recv_sem)
    sums = score_recv[...].reshape(nodes, LANES)
    lane = iota((nodes, LANES), 1) - lax.rem(CAP * n, LANES)
    token_score = jnp.zeros((1, tokens), f32)
    for r in range(CAP):
        column = jnp.sum(jnp.where(lane == r, sums, 0.0), 1, keepdims=True)
        column = jnp.sum(jnp.where(onehot > 0, column, 0.0), 0, keepdims=True)
        token_score += jnp.where(rank == r, column, 0.0)
    score_out[...] = jnp.where(hit, token_score, 0.0)

    settle(others, score_send_sem)
    for k in range(members - 1):
        settle(back_parts.at[k], back_send_sem.at[k])
    for q in range(len(plan)):
        settle(send.at[q, pl.ds(0, nodes - 1)], send_sem.at[q])
        settle(recv.at[q, pl.ds(0, devices - nodes)], pass_send_sem.at[q])


def finish(
    early, scores, hidden_grad, weight, second, weight_decayed, second_decayed, hidden_t, scaled,
    score_out, hidden_out, weight_out, second_out,
    weight_late, second_late, copy_sem,
):
    units, features = weight.shape
    copies = [
        pltpu.make_async_copy(scores, score_out, copy_sem.at[0]),
        pltpu.make_async_copy(hidden_grad, hidden_out, copy_sem.at[1]),
    ]
    pieces = 4
    for i in range(pieces):
        rows = pl.ds(i * (units // pieces), units // pieces)
        for j, (source, target) in enumerate(((weight, weight_out), (second, second_out))):
            copies.append(pltpu.make_async_copy(
                source.at[rows, pl.ds(0, early)], target.at[rows, pl.ds(0, early)],
                copy_sem.at[2 + 2 * i + j],
            ))
    for copy in copies:
        copy.start()
    base = 2 + 2 * pieces
    for i, first in enumerate(range(early, features, WIDTH)):
        columns, late = pl.ds(first, WIDTH), pl.ds(first - early, WIDTH)
        weight_late[:, late], second_late[:, late] = adamw(
            hidden_t[...], scaled[:, columns], weight_decayed[:, columns], second_decayed[:, columns]
        )
        for j, (source, target) in enumerate(((weight_late, weight_out), (second_late, second_out))):
            copies.append(pltpu.make_async_copy(
                source.at[:, late], target.at[:, columns], copy_sem.at[base + 2 * i + j]
            ))
            copies[-1].start()
    for copy in copies:
        copy.wait()


def on_device(nodes, members, grad_out, expert_ids, gate_weights, saved_hidden, down_weight, second_moment):
    tokens, features = grad_out.shape
    _, slots, units = saved_hidden.shape
    chosen = expert_ids.shape[1]
    devices = nodes * members
    group = min(16, nodes)
    half = nodes * CAP
    back_type = f32 if slots * features <= 1 << 20 else bf16
    blocks = [None] + list(range(features // WIDTH))
    plan = [blocks[i:i + BLOCKS] for i in range(0, len(blocks), BLOCKS)]
    chunks = len(plan)
    ahead = features // WIDTH - LATE
    gaps = [0, (4 * ahead) // 7, ahead]
    early = ahead * WIDTH
    small = pl.BlockSpec(memory_space=pltpu.VMEM)
    large = pl.BlockSpec(memory_space=pl.ANY)
    kept = pl.pallas_call(
        functools.partial(kernel, nodes, members, plan, gaps),
        out_shape=(
            pltpu.VMEM((chosen, tokens), f32),
            pltpu.VMEM((slots, units), bf16),
            pltpu.VMEM((units, features), bf16),
            pltpu.VMEM((units, features), bf16),
            pltpu.VMEM((units, features), f32),
            pltpu.VMEM((units, features), f32),
            pltpu.VMEM((units, slots), bf16),
            pltpu.VMEM((slots, features), bf16),
        ),
        in_specs=[large] * 6,
        out_specs=(small,) * 8,
        scratch_shapes=[
            pltpu.VMEM((chosen, tokens), jnp.int32),
            pltpu.VMEM((chosen, tokens), f32),
            pltpu.VMEM((tokens, features), bf16),
            pltpu.VMEM((slots, units), bf16),
            pltpu.VMEM((units, features), bf16),
            pltpu.VMEM((units, features), bf16),
            pltpu.VMEM((chunks, nodes, SLAB, WIDTH), bf16),
            pltpu.VMEM((chunks, devices, SLAB, WIDTH), bf16),
            pltpu.VMEM((BLOCKS * group * CAP, group * SLAB), bf16),
            pltpu.VMEM((slots, features), bf16),
            pltpu.VMEM((slots, WIDTH), f32),
            pltpu.VMEM((slots, units), f32),
            pltpu.VMEM((slots, features), back_type),
            pltpu.VMEM((members - 1, half, features), back_type),
            pltpu.VMEM((half, LANES), f32),
            pltpu.VMEM((-(-half // LANES), 1, LANES), f32),
            pltpu.VMEM((nodes, 1, LANES), f32),
            pltpu.SemaphoreType.DMA((6,)),
            pltpu.SemaphoreType.DMA((chunks,)),
            pltpu.SemaphoreType.DMA((chunks,)),
            pltpu.SemaphoreType.DMA((chunks,)),
            pltpu.SemaphoreType.DMA((chunks,)),
            pltpu.SemaphoreType.DMA((members - 1,)),
            pltpu.SemaphoreType.DMA((members - 1,)),
            pltpu.SemaphoreType.DMA,
            pltpu.SemaphoreType.DMA,
        ],
        compiler_params=pltpu.CompilerParams(
            collective_id=0, has_side_effects=True, vmem_limit_bytes=40 * 1024 * 1024
        ),
        cost_estimate=pl.CostEstimate(
            flops=4 * slots * units * features, bytes_accessed=4 * units * features, transcendentals=0
        ),
    )(expert_ids.T, gate_weights.T, grad_out, saved_hidden[0], down_weight[0], second_moment[0])
    kept = [pltpu.with_memory_space_constraint(a, pltpu.VMEM) for a in kept]
    scores, hidden_grad, new_weight, new_second = pl.pallas_call(
        functools.partial(finish, early),
        out_shape=(
            jax.ShapeDtypeStruct((chosen, tokens), f32),
            jax.ShapeDtypeStruct((slots, units), bf16),
            jax.ShapeDtypeStruct((units, features), bf16),
            jax.ShapeDtypeStruct((units, features), bf16),
        ),
        in_specs=[small] * 8,
        out_specs=(large,) * 4,
        scratch_shapes=[
            pltpu.VMEM((units, features - early), bf16),
            pltpu.VMEM((units, features - early), bf16),
            pltpu.SemaphoreType.DMA((10 + 2 * LATE,)),
        ],
        compiler_params=pltpu.CompilerParams(vmem_limit_bytes=16 * 1024 * 1024),
        cost_estimate=pl.CostEstimate(
            flops=2 * slots * units * LATE * WIDTH, bytes_accessed=4 * units * features, transcendentals=0
        ),
    )(*kept)
    return scores.T, hidden_grad[None], new_weight[None], new_second[None]


def solution(mesh):
    return jax.shard_map(
        functools.partial(on_device, mesh.shape["node"], mesh.shape["local"]),
        mesh=mesh,
        in_specs=(
            P(("node", "local"), None),
            P(("node", "local"), None),
            P(("node", "local"), None),
            P("node", None, "local"),
            P("node", "local", None),
            P("node", "local", None),
        ),
        out_specs=(
            P(("node", "local"), None),
            P("node", None, "local"),
            P("node", "local", None),
            P("node", "local", None),
        ),
        check_vma=False,
    )
```

```python
import functools

import jax
import jax.numpy as jnp
from jax import lax
from jax.experimental import pallas as pl
from jax.experimental.pallas import tpu as pltpu
from jax.sharding import PartitionSpec as P

MESH = pl.DeviceIdType.MESH
EXPERTS_PER_HOST = 4
CAP = 2
WIDTH = 256
SLAB = 16
BLOCKS = SLAB // CAP
LANES = 128
LATE = 9

beta_second = 0.95
learn_rate = 0.002
decay_rate = 0.1
epsilon = 1e-08
correct_second = 0.994079470779666

f32 = jnp.float32
bf16 = jnp.bfloat16


def dot(a, b, dims=((1,), (0,))):
    return lax.dot_general(a, b, (dims, ((), ())), preferred_element_type=f32)


def iota(shape, axis):
    return lax.broadcasted_iota(jnp.int32, shape, axis)


def adamw(hidden_t, scaled, weight, second):
    grad = dot(hidden_t, scaled)
    second_new = second + ((1.0 - beta_second) * grad) * grad
    root = second_new * lax.rsqrt(second_new) + epsilon * correct_second ** 0.5
    step = (learn_rate * correct_second ** 0.5 * grad) * pl.reciprocal(root, approx=True)
    return (weight - step).astype(bf16), second_new.astype(bf16)


def kernel(
    nodes, members, plan, early,
    ids_hbm, gates_hbm, grad_hbm, hidden_hbm, weight_hbm, second_hbm,
    score_out, hidden_out, weight_out, second_out, weight_decayed, second_decayed, hidden_t, scaled,
    ids_ref, gates_ref, grads, hidden, weight, second, send, recv, picks, x, gate,
    unscaled, back, back_parts, score_sums, score_send, score_recv,
    load_sem, send_sem, recv_sem, pass_send_sem, pass_recv_sem,
    back_send_sem, back_recv_sem, score_send_sem, score_recv_sem,
):
    n, l = lax.axis_index("node"), lax.axis_index("local")
    devices = nodes * members
    me = l * nodes + n
    tokens = grads.shape[0]
    slots, units = hidden.shape
    group = min(16, nodes)
    half = nodes * CAP

    loads = [
        pltpu.make_async_copy(source, target, load_sem.at[i])
        for i, (source, target) in enumerate(
            (
                (ids_hbm, ids_ref), (gates_hbm, gates_ref), (grad_hbm, grads),
                (hidden_hbm, hidden), (weight_hbm, weight), (second_hbm, second),
            )
        )
    ]
    for load in loads[:3]:
        load.start()

    barrier = pltpu.get_barrier_semaphore()

    def greet(k, carry):
        pl.semaphore_signal(
            barrier, inc=1, device_id=(lax.rem(n + k, nodes), l), device_id_type=MESH
        )
        return carry

    lax.fori_loop(1, nodes, greet, 0, unroll=nodes <= 16)
    siblings = [(n, lax.rem(l + k, members)) for k in range(1, members)]
    for sibling in siblings:
        pl.semaphore_signal(barrier, inc=1, device_id=sibling, device_id_type=MESH)

    loads[0].wait()
    loads[1].wait()
    ids = ids_ref[...]
    hit = ids % EXPERTS_PER_HOST == 0
    hit_one = jnp.where(hit, 1, 0)
    present = jnp.max(hit_one, 0, keepdims=True)
    dest = jnp.sum(jnp.where(hit, ids // EXPERTS_PER_HOST, 0), 0, keepdims=True)
    dest = jnp.where(present > 0, dest, -1)
    onehot = jnp.where(iota((nodes, tokens), 0) == dest, 1.0, 0.0).astype(f32)
    before = jnp.where(iota((tokens, tokens), 0) < iota((tokens, tokens), 1), 1.0, 0.0)
    earlier = dot(onehot.astype(bf16), before.astype(bf16))
    rank = jnp.sum(onehot * earlier, 0, keepdims=True).astype(jnp.int32)
    key = jnp.where(present > 0, dest * SLAB + rank, -SLAB * CAP)
    matched = jnp.sum(jnp.where(hit, gates_ref[...], 0.0), 0, keepdims=True)
    matched = matched.astype(bf16).astype(f32)

    loads[2].wait()
    for load in loads[3:]:
        load.start()
    place = iota((nodes * SLAB, tokens), 0)

    def pack(q):
        total = None
        for c in range(0, len(plan[q]), 2):
            masks, rights = [], []
            for block in plan[q][c:c + 2]:
                mask = place == key + CAP * (c + len(masks))
                if block is None:
                    masks.append(jnp.where(mask, matched, 0.0).astype(bf16))
                    rights.append(jnp.ones((tokens, WIDTH), bf16))
                else:
                    masks.append(jnp.where(mask, 1.0, 0.0).astype(bf16))
                    rights.append(grads[:, block * WIDTH:(block + 1) * WIDTH])
            part = dot(jnp.concatenate(masks, 1), jnp.concatenate(rights, 0))
            total = part if total is None else total + part
        send[q] = total.astype(bf16).reshape(nodes, SLAB, WIDTH)

    def turn(i):
        return nodes // 2 + ((i + 1) // 2) * (1 - 2 * lax.rem(i, 2))

    def push(q):
        def one(i, carry):
            other = lax.rem(n + turn(i), nodes)
            pltpu.make_async_remote_copy(
                src_ref=send.at[q, other], dst_ref=recv.at[q, me],
                send_sem=send_sem.at[q], recv_sem=recv_sem.at[q],
                device_id=(other, l), device_id_type=MESH,
            ).start()
            return carry

        lax.fori_loop(0, nodes - 1, one, 0, unroll=nodes <= 16)
        recv[q, me] = send[q, n]

    def settle(ref, sem):
        pltpu.make_async_copy(ref, ref, sem).wait()

    def relay(q):
        settle(recv.at[q, pl.ds(0, nodes - 1)], recv_sem.at[q])
        mine = recv.at[q, pl.ds(l * nodes, nodes)]
        for sibling in siblings:
            pltpu.make_async_remote_copy(
                src_ref=mine, dst_ref=mine,
                send_sem=pass_send_sem.at[q], recv_sem=pass_recv_sem.at[q],
                device_id=sibling, device_id_type=MESH,
            ).start()

    def collect(q):
        settle(recv.at[q, pl.ds(0, devices - nodes)], pass_recv_sem.at[q])

    def unpack(q, member, scored=False):
        rows = group * CAP
        for g in range(nodes // group):
            source = member * nodes + g * group
            landed = recv[q, pl.ds(source, group)].reshape(group * SLAB, WIDTH)
            chosen = dot(picks[...], landed)
            here = pl.ds(pl.multiple_of(source * CAP, rows), rows)
            local = slice(g * rows, (g + 1) * rows)
            if None in plan[q]:
                c = plan[q].index(None)
                gate[here, :] = chosen[c * rows:(c + 1) * rows]
            factor = gate[here, :]
            sums = None
            for c, block in enumerate(plan[q]):
                if block is None:
                    continue
                part = chosen[c * rows:(c + 1) * rows]
                columns = slice(block * WIDTH, (block + 1) * WIDTH)
                x[here, columns] = part.astype(bf16)
                scaled[here, columns] = (factor * part).astype(bf16)
                if scored:
                    against = back[here, columns].astype(f32)
                    for k in range(members - 1):
                        against += back_parts[k, local, columns].astype(f32)
                    term = part * against
                    sums = term if sums is None else sums + term
            if scored:
                sums = sums[:, :LANES] + sums[:, LANES:]
                score_sums[local, :] = sums if q == 0 else score_sums[local, :] + sums

    def span(q):
        blocks = [b for b in plan[q] if b is not None]
        return blocks[0] * WIDTH, (blocks[-1] + 1) * WIDTH

    def multiply(q):
        first, last = span(q)
        part = dot(weight[:, first:last], x[:, first:last], ((1,), (1,)))
        unscaled[...] = part if q == 0 else unscaled[...] + part

    def decay():
        def tile(i, carry):
            columns = pl.ds(pl.multiple_of(i * WIDTH, WIDTH), WIDTH)
            weight_decayed[:, columns] = weight[:, columns].astype(f32) * (1.0 - learn_rate * decay_rate)
            second_decayed[:, columns] = second[:, columns].astype(f32) * beta_second
            return carry

        lax.fori_loop(0, weight.shape[1] // WIDTH, tile, 0)

    def update(first, last):
        def tile(i, carry):
            columns = pl.ds(pl.multiple_of(i * WIDTH, WIDTH), WIDTH)
            weight_out[:, columns], second_out[:, columns] = adamw(
                hidden_t[...], scaled[:, columns], weight_decayed[:, columns], second_decayed[:, columns]
            )
            return carry

        lax.fori_loop(first, last, tile, 0)

    pack(0)
    pl.semaphore_wait(barrier, nodes - 1 + members - 1)
    push(0)
    for q in range(1, len(plan)):
        pack(q)
        push(q)
    loads[3].wait()
    loads[4].wait()
    features = weight.shape[1]
    stripe = 2 * WIDTH
    for j in range(0, features, stripe):
        back[:, j:j + stripe] = dot(hidden[...], weight[:, j:j + stripe]).astype(back.dtype)
    for k in range(1, members):
        other = lax.rem(l + k, members)
        pltpu.make_async_remote_copy(
            src_ref=back.at[pl.ds(pl.multiple_of(other * half, half), half)], dst_ref=back_parts.at[k - 1],
            send_sem=back_send_sem.at[k - 1], recv_sem=back_recv_sem.at[k - 1],
            device_id=(n, other), device_id_type=MESH,
        ).start()

    picked_row, picked_col = iota((group * CAP, group * SLAB), 0), iota((group * CAP, group * SLAB), 1)
    wanted = (picked_row // CAP) * SLAB + picked_row % CAP
    for c in range(BLOCKS):
        picks[c * group * CAP:(c + 1) * group * CAP, :] = jnp.where(
            picked_col == wanted + CAP * c, 1.0, 0.0
        ).astype(bf16)
    hidden_t[...] = hidden[...].astype(f32).T.astype(bf16)
    loads[5].wait()

    decay()

    for k in range(members - 1):
        settle(back_parts.at[k], back_recv_sem.at[k])
    for q in range(len(plan)):
        relay(q)
        unpack(q, l, scored=True)
        if q == len(plan) - 1:
            for s in range(0, half, LANES):
                part = score_sums[s:min(s + LANES, half), :]
                if part.shape[0] < LANES:
                    part = jnp.concatenate([part, jnp.zeros((LANES - part.shape[0], LANES), f32)], 0)
                score_send[s // LANES] = jnp.sum(part.T, 0, keepdims=True)

            def answer(i, carry):
                other = lax.rem(n + turn(i), nodes)
                pltpu.make_async_remote_copy(
                    src_ref=score_send.at[(CAP * other) // LANES], dst_ref=score_recv.at[n],
                    send_sem=score_send_sem, recv_sem=score_recv_sem,
                    device_id=(other, l), device_id_type=MESH,
                ).start()
                return carry

            lax.fori_loop(0, nodes - 1, answer, 0, unroll=nodes <= 16)
            score_recv[n] = score_send[(CAP * n) // LANES]
        collect(q)
        for k in range(1, members):
            unpack(q, lax.rem(l + k, members))
        multiply(q)
        if q < len(plan) - 1:
            update(early[q], early[q + 1])

    raw = unscaled[...].T
    for j in range(0, units, LANES):
        hidden_out[:, j:j + LANES] = (gate[:, :LANES] * raw[:, j:j + LANES]).astype(bf16)
    update(early[-2], early[-1])

    others = score_recv.at[pl.ds(0, nodes - 1)]
    settle(others, score_recv_sem)
    sums = score_recv[...].reshape(nodes, LANES)
    lane = iota((nodes, LANES), 1) - lax.rem(CAP * n, LANES)
    token_score = jnp.zeros((1, tokens), f32)
    for r in range(CAP):
        column = jnp.sum(jnp.where(lane == r, sums, 0.0), 1, keepdims=True)
        column = jnp.sum(jnp.where(onehot > 0, column, 0.0), 0, keepdims=True)
        token_score += jnp.where(rank == r, column, 0.0)
    score_out[...] = jnp.where(hit, token_score, 0.0)

    settle(others, score_send_sem)
    for k in range(members - 1):
        settle(back_parts.at[k], back_send_sem.at[k])
    for q in range(len(plan)):
        settle(send.at[q, pl.ds(0, nodes - 1)], send_sem.at[q])
        settle(recv.at[q, pl.ds(0, devices - nodes)], pass_send_sem.at[q])


def finish(
    early, scores, hidden_grad, weight, second, weight_decayed, second_decayed, hidden_t, scaled,
    score_out, hidden_out, weight_out, second_out,
    weight_late, second_late, copy_sem,
):
    units, features = weight.shape
    copies = [
        pltpu.make_async_copy(scores, score_out, copy_sem.at[0]),
        pltpu.make_async_copy(hidden_grad, hidden_out, copy_sem.at[1]),
    ]
    pieces = 4
    for i in range(pieces):
        rows = pl.ds(i * (units // pieces), units // pieces)
        for j, (source, target) in enumerate(((weight, weight_out), (second, second_out))):
            copies.append(pltpu.make_async_copy(
                source.at[rows, pl.ds(0, early)], target.at[rows, pl.ds(0, early)],
                copy_sem.at[2 + 2 * i + j],
            ))
    for copy in copies:
        copy.start()
    base = 2 + 2 * pieces
    for i, first in enumerate(range(early, features, WIDTH)):
        columns, late = pl.ds(first, WIDTH), pl.ds(first - early, WIDTH)
        weight_late[:, late], second_late[:, late] = adamw(
            hidden_t[...], scaled[:, columns], weight_decayed[:, columns], second_decayed[:, columns]
        )
        for j, (source, target) in enumerate(((weight_late, weight_out), (second_late, second_out))):
            copies.append(pltpu.make_async_copy(
                source.at[:, late], target.at[:, columns], copy_sem.at[base + 2 * i + j]
            ))
            copies[-1].start()
    for copy in copies:
        copy.wait()


def on_device(nodes, members, grad_out, expert_ids, gate_weights, saved_hidden, down_weight, second_moment):
    tokens, features = grad_out.shape
    _, slots, units = saved_hidden.shape
    chosen = expert_ids.shape[1]
    devices = nodes * members
    group = min(16, nodes)
    half = nodes * CAP
    back_type = f32 if slots * features <= 1 << 20 else bf16
    blocks = [None] + list(range(features // WIDTH))
    plan = [blocks[i:i + BLOCKS] for i in range(0, len(blocks), BLOCKS)]
    chunks = len(plan)
    ahead = features // WIDTH - LATE
    gaps = [0, (4 * ahead) // 5, ahead]
    early = ahead * WIDTH
    small = pl.BlockSpec(memory_space=pltpu.VMEM)
    large = pl.BlockSpec(memory_space=pl.ANY)
    kept = pl.pallas_call(
        functools.partial(kernel, nodes, members, plan, gaps),
        out_shape=(
            pltpu.VMEM((chosen, tokens), f32),
            pltpu.VMEM((slots, units), bf16),
            pltpu.VMEM((units, features), bf16),
            pltpu.VMEM((units, features), bf16),
            pltpu.VMEM((units, features), f32),
            pltpu.VMEM((units, features), f32),
            pltpu.VMEM((units, slots), bf16),
            pltpu.VMEM((slots, features), bf16),
        ),
        in_specs=[large] * 6,
        out_specs=(small,) * 8,
        scratch_shapes=[
            pltpu.VMEM((chosen, tokens), jnp.int32),
            pltpu.VMEM((chosen, tokens), f32),
            pltpu.VMEM((tokens, features), bf16),
            pltpu.VMEM((slots, units), bf16),
            pltpu.VMEM((units, features), bf16),
            pltpu.VMEM((units, features), bf16),
            pltpu.VMEM((chunks, nodes, SLAB, WIDTH), bf16),
            pltpu.VMEM((chunks, devices, SLAB, WIDTH), bf16),
            pltpu.VMEM((BLOCKS * group * CAP, group * SLAB), bf16),
            pltpu.VMEM((slots, features), bf16),
            pltpu.VMEM((slots, WIDTH), f32),
            pltpu.VMEM((units, slots), f32),
            pltpu.VMEM((slots, features), back_type),
            pltpu.VMEM((members - 1, half, features), back_type),
            pltpu.VMEM((half, LANES), f32),
            pltpu.VMEM((-(-half // LANES), 1, LANES), f32),
            pltpu.VMEM((nodes, 1, LANES), f32),
            pltpu.SemaphoreType.DMA((6,)),
            pltpu.SemaphoreType.DMA((chunks,)),
            pltpu.SemaphoreType.DMA((chunks,)),
            pltpu.SemaphoreType.DMA((chunks,)),
            pltpu.SemaphoreType.DMA((chunks,)),
            pltpu.SemaphoreType.DMA((members - 1,)),
            pltpu.SemaphoreType.DMA((members - 1,)),
            pltpu.SemaphoreType.DMA,
            pltpu.SemaphoreType.DMA,
        ],
        compiler_params=pltpu.CompilerParams(
            collective_id=0, has_side_effects=True, vmem_limit_bytes=40 * 1024 * 1024
        ),
        cost_estimate=pl.CostEstimate(
            flops=4 * slots * units * features, bytes_accessed=4 * units * features, transcendentals=0
        ),
    )(expert_ids.T, gate_weights.T, grad_out, saved_hidden[0], down_weight[0], second_moment[0])
    kept = [pltpu.with_memory_space_constraint(a, pltpu.VMEM) for a in kept]
    scores, hidden_grad, new_weight, new_second = pl.pallas_call(
        functools.partial(finish, early),
        out_shape=(
            jax.ShapeDtypeStruct((chosen, tokens), f32),
            jax.ShapeDtypeStruct((slots, units), bf16),
            jax.ShapeDtypeStruct((units, features), bf16),
            jax.ShapeDtypeStruct((units, features), bf16),
        ),
        in_specs=[small] * 8,
        out_specs=(large,) * 4,
        scratch_shapes=[
            pltpu.VMEM((units, features - early), bf16),
            pltpu.VMEM((units, features - early), bf16),
            pltpu.SemaphoreType.DMA((10 + 2 * LATE,)),
        ],
        compiler_params=pltpu.CompilerParams(vmem_limit_bytes=16 * 1024 * 1024),
        cost_estimate=pl.CostEstimate(
            flops=2 * slots * units * LATE * WIDTH, bytes_accessed=4 * units * features, transcendentals=0
        ),
    )(*kept)
    return scores.T, hidden_grad[None], new_weight[None], new_second[None]


def solution(mesh):
    return jax.shard_map(
        functools.partial(on_device, mesh.shape["node"], mesh.shape["local"]),
        mesh=mesh,
        in_specs=(
            P(("node", "local"), None),
            P(("node", "local"), None),
            P(("node", "local"), None),
            P("node", None, "local"),
            P("node", "local", None),
            P("node", "local", None),
        ),
        out_specs=(
            P(("node", "local"), None),
            P("node", None, "local"),
            P("node", "local", None),
            P("node", "local", None),
        ),
        check_vma=False,
    )
```

```python
import functools

import jax
import jax.numpy as jnp
from jax import lax
from jax.experimental import pallas as pl
from jax.experimental.pallas import tpu as pltpu
from jax.sharding import PartitionSpec as P

MESH = pl.DeviceIdType.MESH
EXPERTS_PER_HOST = 4
CAP = 2
WIDTH = 256
SLAB = 16
BLOCKS = SLAB // CAP
LANES = 128
LATE = 2

beta_second = 0.95
learn_rate = 0.002
decay_rate = 0.1
epsilon = 1e-08
correct_second = 0.994079470779666

f32 = jnp.float32
bf16 = jnp.bfloat16


def dot(a, b, dims=((1,), (0,))):
    return lax.dot_general(a, b, (dims, ((), ())), preferred_element_type=f32)


def iota(shape, axis):
    return lax.broadcasted_iota(jnp.int32, shape, axis)


def adamw(hidden_t, scaled, weight, second):
    grad = dot(hidden_t, scaled)
    second_new = second + ((1.0 - beta_second) * grad) * grad
    root = second_new * lax.rsqrt(second_new) + epsilon * correct_second ** 0.5
    step = (learn_rate * correct_second ** 0.5 * grad) * pl.reciprocal(root, approx=True)
    return (weight - step).astype(bf16), second_new.astype(bf16)


def kernel(
    nodes, members, plan, early,
    ids_hbm, gates_hbm, grad_hbm, hidden_hbm, weight_hbm, second_hbm,
    score_out, hidden_out, weight_out, second_out, weight_decayed, second_decayed, hidden_t, scaled,
    ids_ref, gates_ref, grads, hidden, weight, second, send, recv, picks, x, gate,
    unscaled, back, back_parts, score_sums, score_send, score_recv,
    load_sem, send_sem, recv_sem, pass_send_sem, pass_recv_sem,
    back_send_sem, back_recv_sem, score_send_sem, score_recv_sem,
):
    n, l = lax.axis_index("node"), lax.axis_index("local")
    devices = nodes * members
    me = l * nodes + n
    tokens = grads.shape[0]
    slots, units = hidden.shape
    group = min(16, nodes)
    half = nodes * CAP

    loads = [
        pltpu.make_async_copy(source, target, load_sem.at[i])
        for i, (source, target) in enumerate(
            (
                (ids_hbm, ids_ref), (gates_hbm, gates_ref), (grad_hbm, grads),
                (hidden_hbm, hidden), (weight_hbm, weight), (second_hbm, second),
            )
        )
    ]
    barrier = pltpu.get_barrier_semaphore()

    def greet(k, carry):
        pl.semaphore_signal(
            barrier, inc=1, device_id=(lax.rem(n + k, nodes), l), device_id_type=MESH
        )
        return carry

    lax.fori_loop(1, nodes, greet, 0, unroll=nodes <= 16)
    siblings = [(n, lax.rem(l + k, members)) for k in range(1, members)]
    for sibling in siblings:
        pl.semaphore_signal(barrier, inc=1, device_id=sibling, device_id_type=MESH)

    for load in loads[:3]:
        load.start()
    loads[0].wait()
    loads[1].wait()
    ids = ids_ref[...]
    hit = ids % EXPERTS_PER_HOST == 0
    hit_one = jnp.where(hit, 1, 0)
    present = jnp.max(hit_one, 0, keepdims=True)
    dest = jnp.sum(jnp.where(hit, ids // EXPERTS_PER_HOST, 0), 0, keepdims=True)
    dest = jnp.where(present > 0, dest, -1)
    onehot = jnp.where(iota((nodes, tokens), 0) == dest, 1.0, 0.0).astype(f32)
    before = jnp.where(iota((tokens, tokens), 0) < iota((tokens, tokens), 1), 1.0, 0.0)
    earlier = dot(onehot.astype(bf16), before.astype(bf16))
    rank = jnp.sum(onehot * earlier, 0, keepdims=True).astype(jnp.int32)
    key = jnp.where(present > 0, dest * SLAB + rank, -SLAB * CAP)
    matched = jnp.sum(jnp.where(hit, gates_ref[...], 0.0), 0, keepdims=True)
    matched = matched.astype(bf16).astype(f32)

    loads[2].wait()
    for load in loads[3:]:
        load.start()
    place = iota((nodes * SLAB, tokens), 0)

    def pack(q):
        total = None
        for c in range(0, len(plan[q]), 2):
            masks, rights = [], []
            for block in plan[q][c:c + 2]:
                mask = place == key + CAP * (c + len(masks))
                if block is None:
                    masks.append(jnp.where(mask, matched, 0.0).astype(bf16))
                    rights.append(jnp.ones((tokens, WIDTH), bf16))
                else:
                    masks.append(jnp.where(mask, 1.0, 0.0).astype(bf16))
                    rights.append(grads[:, block * WIDTH:(block + 1) * WIDTH])
            part = dot(jnp.concatenate(masks, 1), jnp.concatenate(rights, 0))
            total = part if total is None else total + part
        send[q] = total.astype(bf16).reshape(nodes, SLAB, WIDTH)

    def turn(i):
        return nodes // 2 + ((i + 1) // 2) * (1 - 2 * lax.rem(i, 2))

    def push(q):
        def one(i, carry):
            other = lax.rem(n + turn(i), nodes)
            pltpu.make_async_remote_copy(
                src_ref=send.at[q, other], dst_ref=recv.at[q, me],
                send_sem=send_sem.at[q], recv_sem=recv_sem.at[q],
                device_id=(other, l), device_id_type=MESH,
            ).start()
            return carry

        lax.fori_loop(0, nodes - 1, one, 0, unroll=nodes <= 16)
        recv[q, me] = send[q, n]

    def settle(ref, sem):
        pltpu.make_async_copy(ref, ref, sem).wait()

    def relay(q):
        settle(recv.at[q, pl.ds(0, nodes - 1)], recv_sem.at[q])
        mine = recv.at[q, pl.ds(l * nodes, nodes)]
        for sibling in siblings:
            pltpu.make_async_remote_copy(
                src_ref=mine, dst_ref=mine,
                send_sem=pass_send_sem.at[q], recv_sem=pass_recv_sem.at[q],
                device_id=sibling, device_id_type=MESH,
            ).start()

    def collect(q):
        settle(recv.at[q, pl.ds(0, devices - nodes)], pass_recv_sem.at[q])

    def unpack(q, member, scored=False):
        rows = group * CAP
        for g in range(nodes // group):
            source = member * nodes + g * group
            landed = recv[q, pl.ds(source, group)].reshape(group * SLAB, WIDTH)
            chosen = dot(picks[...], landed)
            here = pl.ds(pl.multiple_of(source * CAP, rows), rows)
            local = slice(g * rows, (g + 1) * rows)
            if None in plan[q]:
                c = plan[q].index(None)
                gate[here, :] = chosen[c * rows:(c + 1) * rows]
            factor = gate[here, :]
            sums = None
            for c, block in enumerate(plan[q]):
                if block is None:
                    continue
                part = chosen[c * rows:(c + 1) * rows]
                columns = slice(block * WIDTH, (block + 1) * WIDTH)
                x[here, columns] = part.astype(bf16)
                scaled[here, columns] = (factor * part).astype(bf16)
                if scored:
                    against = back[here, columns].astype(f32)
                    for k in range(members - 1):
                        against += back_parts[k, local, columns].astype(f32)
                    term = part * against
                    sums = term if sums is None else sums + term
            if scored:
                sums = sums[:, :LANES] + sums[:, LANES:]
                score_sums[local, :] = sums if q == 0 else score_sums[local, :] + sums

    def span(q):
        blocks = [b for b in plan[q] if b is not None]
        return blocks[0] * WIDTH, (blocks[-1] + 1) * WIDTH

    def multiply(q):
        first, last = span(q)
        part = dot(weight[:, first:last], x[:, first:last], ((1,), (1,)))
        unscaled[...] = part if q == 0 else unscaled[...] + part

    def decay():
        def tile(i, carry):
            columns = pl.ds(pl.multiple_of(i * WIDTH, WIDTH), WIDTH)
            weight_decayed[:, columns] = weight[:, columns].astype(f32) * (1.0 - learn_rate * decay_rate)
            second_decayed[:, columns] = second[:, columns].astype(f32) * beta_second
            return carry

        lax.fori_loop(0, weight.shape[1] // WIDTH, tile, 0)

    def update(first, last):
        def tile(i, carry):
            columns = pl.ds(pl.multiple_of(i * WIDTH, WIDTH), WIDTH)
            weight_out[:, columns], second_out[:, columns] = adamw(
                hidden_t[...], scaled[:, columns], weight_decayed[:, columns], second_decayed[:, columns]
            )
            return carry

        lax.fori_loop(first, last, tile, 0)

    pack(0)
    pl.semaphore_wait(barrier, nodes - 1 + members - 1)
    push(0)
    for q in range(1, len(plan)):
        pack(q)
        push(q)
    loads[3].wait()
    loads[4].wait()
    features = weight.shape[1]
    stripe = 2 * WIDTH
    for j in range(0, features, stripe):
        back[:, j:j + stripe] = dot(hidden[...], weight[:, j:j + stripe]).astype(back.dtype)
    for k in range(1, members):
        other = lax.rem(l + k, members)
        pltpu.make_async_remote_copy(
            src_ref=back.at[pl.ds(pl.multiple_of(other * half, half), half)], dst_ref=back_parts.at[k - 1],
            send_sem=back_send_sem.at[k - 1], recv_sem=back_recv_sem.at[k - 1],
            device_id=(n, other), device_id_type=MESH,
        ).start()

    picked_row, picked_col = iota((group * CAP, group * SLAB), 0), iota((group * CAP, group * SLAB), 1)
    wanted = (picked_row // CAP) * SLAB + picked_row % CAP
    for c in range(BLOCKS):
        picks[c * group * CAP:(c + 1) * group * CAP, :] = jnp.where(
            picked_col == wanted + CAP * c, 1.0, 0.0
        ).astype(bf16)
    hidden_t[...] = hidden[...].astype(f32).T.astype(bf16)
    loads[5].wait()

    decay()

    for k in range(members - 1):
        settle(back_parts.at[k], back_recv_sem.at[k])
    for q in range(len(plan)):
        relay(q)
        unpack(q, l, scored=True)
        if q == len(plan) - 1:
            for s in range(0, half, LANES):
                part = score_sums[s:min(s + LANES, half), :]
                if part.shape[0] < LANES:
                    part = jnp.concatenate([part, jnp.zeros((LANES - part.shape[0], LANES), f32)], 0)
                score_send[s // LANES] = jnp.sum(part.T, 0, keepdims=True)

            def answer(i, carry):
                other = lax.rem(n + turn(i), nodes)
                pltpu.make_async_remote_copy(
                    src_ref=score_send.at[(CAP * other) // LANES], dst_ref=score_recv.at[n],
                    send_sem=score_send_sem, recv_sem=score_recv_sem,
                    device_id=(other, l), device_id_type=MESH,
                ).start()
                return carry

            lax.fori_loop(0, nodes - 1, answer, 0, unroll=nodes <= 16)
            score_recv[n] = score_send[(CAP * n) // LANES]
        collect(q)
        for k in range(1, members):
            unpack(q, lax.rem(l + k, members))
        multiply(q)
        if q < len(plan) - 1:
            update(early[q], early[q + 1])

    raw = unscaled[...].T
    for j in range(0, units, LANES):
        hidden_out[:, j:j + LANES] = (gate[:, :LANES] * raw[:, j:j + LANES]).astype(bf16)
    update(early[-2], early[-1])

    others = score_recv.at[pl.ds(0, nodes - 1)]
    settle(others, score_recv_sem)
    sums = score_recv[...].reshape(nodes, LANES)
    lane = iota((nodes, LANES), 1) - lax.rem(CAP * n, LANES)
    token_score = jnp.zeros((1, tokens), f32)
    for r in range(CAP):
        column = jnp.sum(jnp.where(lane == r, sums, 0.0), 1, keepdims=True)
        column = jnp.sum(jnp.where(onehot > 0, column, 0.0), 0, keepdims=True)
        token_score += jnp.where(rank == r, column, 0.0)
    score_out[...] = jnp.where(hit, token_score, 0.0)

    settle(others, score_send_sem)
    for k in range(members - 1):
        settle(back_parts.at[k], back_send_sem.at[k])
    for q in range(len(plan)):
        settle(send.at[q, pl.ds(0, nodes - 1)], send_sem.at[q])
        settle(recv.at[q, pl.ds(0, devices - nodes)], pass_send_sem.at[q])


def finish(
    early, scores, hidden_grad, weight, second, weight_decayed, second_decayed, hidden_t, scaled,
    score_out, hidden_out, weight_out, second_out,
    weight_late, second_late, copy_sem,
):
    units, features = weight.shape
    copies = [
        pltpu.make_async_copy(scores, score_out, copy_sem.at[0]),
        pltpu.make_async_copy(hidden_grad, hidden_out, copy_sem.at[1]),
    ]
    pieces = 4
    for i in range(pieces):
        rows = pl.ds(i * (units // pieces), units // pieces)
        for j, (source, target) in enumerate(((weight, weight_out), (second, second_out))):
            copies.append(pltpu.make_async_copy(
                source.at[rows, pl.ds(0, early)], target.at[rows, pl.ds(0, early)],
                copy_sem.at[2 + 2 * i + j],
            ))
    for copy in copies:
        copy.start()
    base = 2 + 2 * pieces
    for i, first in enumerate(range(early, features, WIDTH)):
        columns, late = pl.ds(first, WIDTH), pl.ds(first - early, WIDTH)
        weight_late[:, late], second_late[:, late] = adamw(
            hidden_t[...], scaled[:, columns], weight_decayed[:, columns], second_decayed[:, columns]
        )
        for j, (source, target) in enumerate(((weight_late, weight_out), (second_late, second_out))):
            copies.append(pltpu.make_async_copy(
                source.at[:, late], target.at[:, columns], copy_sem.at[base + 2 * i + j]
            ))
            copies[-1].start()
    for copy in copies:
        copy.wait()


def on_device(nodes, members, grad_out, expert_ids, gate_weights, saved_hidden, down_weight, second_moment):
    tokens, features = grad_out.shape
    _, slots, units = saved_hidden.shape
    chosen = expert_ids.shape[1]
    devices = nodes * members
    group = min(16, nodes)
    half = nodes * CAP
    back_type = f32 if slots * features <= 1 << 20 else bf16
    blocks = [None] + list(range(features // WIDTH))
    plan = [blocks[i:i + BLOCKS] for i in range(0, len(blocks), BLOCKS)]
    chunks = len(plan)
    ahead = features // WIDTH - LATE
    gaps = [0, (5 * ahead) // 12, ahead]
    early = ahead * WIDTH
    small = pl.BlockSpec(memory_space=pltpu.VMEM)
    large = pl.BlockSpec(memory_space=pl.ANY)
    kept = pl.pallas_call(
        functools.partial(kernel, nodes, members, plan, gaps),
        out_shape=(
            pltpu.VMEM((chosen, tokens), f32),
            pltpu.VMEM((slots, units), bf16),
            pltpu.VMEM((units, features), bf16),
            pltpu.VMEM((units, features), bf16),
            pltpu.VMEM((units, features), f32),
            pltpu.VMEM((units, features), f32),
            pltpu.VMEM((units, slots), bf16),
            pltpu.VMEM((slots, features), bf16),
        ),
        in_specs=[large] * 6,
        out_specs=(small,) * 8,
        scratch_shapes=[
            pltpu.VMEM((chosen, tokens), jnp.int32),
            pltpu.VMEM((chosen, tokens), f32),
            pltpu.VMEM((tokens, features), bf16),
            pltpu.VMEM((slots, units), bf16),
            pltpu.VMEM((units, features), bf16),
            pltpu.VMEM((units, features), bf16),
            pltpu.VMEM((chunks, nodes, SLAB, WIDTH), bf16),
            pltpu.VMEM((chunks, devices, SLAB, WIDTH), bf16),
            pltpu.VMEM((BLOCKS * group * CAP, group * SLAB), bf16),
            pltpu.VMEM((slots, features), bf16),
            pltpu.VMEM((slots, WIDTH), f32),
            pltpu.VMEM((units, slots), f32),
            pltpu.VMEM((slots, features), back_type),
            pltpu.VMEM((members - 1, half, features), back_type),
            pltpu.VMEM((half, LANES), f32),
            pltpu.VMEM((-(-half // LANES), 1, LANES), f32),
            pltpu.VMEM((nodes, 1, LANES), f32),
            pltpu.SemaphoreType.DMA((6,)),
            pltpu.SemaphoreType.DMA((chunks,)),
            pltpu.SemaphoreType.DMA((chunks,)),
            pltpu.SemaphoreType.DMA((chunks,)),
            pltpu.SemaphoreType.DMA((chunks,)),
            pltpu.SemaphoreType.DMA((members - 1,)),
            pltpu.SemaphoreType.DMA((members - 1,)),
            pltpu.SemaphoreType.DMA,
            pltpu.SemaphoreType.DMA,
        ],
        compiler_params=pltpu.CompilerParams(
            collective_id=0, has_side_effects=True, vmem_limit_bytes=40 * 1024 * 1024
        ),
        cost_estimate=pl.CostEstimate(
            flops=4 * slots * units * features, bytes_accessed=4 * units * features, transcendentals=0
        ),
    )(expert_ids.T, gate_weights.T, grad_out, saved_hidden[0], down_weight[0], second_moment[0])
    kept = [pltpu.with_memory_space_constraint(a, pltpu.VMEM) for a in kept]
    scores, hidden_grad, new_weight, new_second = pl.pallas_call(
        functools.partial(finish, early),
        out_shape=(
            jax.ShapeDtypeStruct((chosen, tokens), f32),
            jax.ShapeDtypeStruct((slots, units), bf16),
            jax.ShapeDtypeStruct((units, features), bf16),
            jax.ShapeDtypeStruct((units, features), bf16),
        ),
        in_specs=[small] * 8,
        out_specs=(large,) * 4,
        scratch_shapes=[
            pltpu.VMEM((units, features - early), bf16),
            pltpu.VMEM((units, features - early), bf16),
            pltpu.SemaphoreType.DMA((10 + 2 * LATE,)),
        ],
        compiler_params=pltpu.CompilerParams(vmem_limit_bytes=16 * 1024 * 1024),
        cost_estimate=pl.CostEstimate(
            flops=2 * slots * units * LATE * WIDTH, bytes_accessed=4 * units * features, transcendentals=0
        ),
    )(*kept)
    return scores.T, hidden_grad[None], new_weight[None], new_second[None]


def solution(mesh):
    return jax.shard_map(
        functools.partial(on_device, mesh.shape["node"], mesh.shape["local"]),
        mesh=mesh,
        in_specs=(
            P(("node", "local"), None),
            P(("node", "local"), None),
            P(("node", "local"), None),
            P("node", None, "local"),
            P("node", "local", None),
            P("node", "local", None),
        ),
        out_specs=(
            P(("node", "local"), None),
            P("node", None, "local"),
            P("node", "local", None),
            P("node", "local", None),
        ),
        check_vma=False,
    )
```

```python
import functools

import jax
import jax.numpy as jnp
from jax import lax
from jax.experimental import pallas as pl
from jax.experimental.pallas import tpu as pltpu
from jax.sharding import PartitionSpec as P

MESH = pl.DeviceIdType.MESH
EXPERTS_PER_HOST = 4
CAP = 2
WIDTH = 256
SLAB = 16
BLOCKS = SLAB // CAP
LANES = 128
LATE = 7

beta_second = 0.95
learn_rate = 0.002
decay_rate = 0.1
epsilon = 1e-08
correct_second = 0.994079470779666

f32 = jnp.float32
bf16 = jnp.bfloat16


def dot(a, b, dims=((1,), (0,))):
    return lax.dot_general(a, b, (dims, ((), ())), preferred_element_type=f32)


def iota(shape, axis):
    return lax.broadcasted_iota(jnp.int32, shape, axis)


def adamw(hidden_t, scaled, weight, second):
    grad = dot(hidden_t, scaled)
    second_new = second + ((1.0 - beta_second) * grad) * grad
    root = second_new * lax.rsqrt(second_new) + epsilon * correct_second ** 0.5
    step = (learn_rate * correct_second ** 0.5 * grad) * pl.reciprocal(root, approx=True)
    return (weight - step).astype(bf16), second_new.astype(bf16)


def kernel(
    nodes, members, plan, early,
    ids_hbm, gates_hbm, grad_hbm, hidden_hbm, weight_hbm, second_hbm,
    score_out, hidden_out, weight_out, second_out, weight_decayed, second_decayed, hidden_t, scaled,
    ids_ref, gates_ref, grads, hidden, weight, second, send, recv, picks, x, gate,
    unscaled, back, back_parts, score_sums, score_send, score_recv,
    load_sem, send_sem, recv_sem, pass_send_sem, pass_recv_sem,
    back_send_sem, back_recv_sem, score_send_sem, score_recv_sem,
):
    n, l = lax.axis_index("node"), lax.axis_index("local")
    devices = nodes * members
    me = l * nodes + n
    tokens = grads.shape[0]
    slots, units = hidden.shape
    group = min(16, nodes)
    half = nodes * CAP

    loads = [
        pltpu.make_async_copy(source, target, load_sem.at[i])
        for i, (source, target) in enumerate(
            (
                (ids_hbm, ids_ref), (gates_hbm, gates_ref), (grad_hbm, grads),
                (hidden_hbm, hidden), (weight_hbm, weight), (second_hbm, second),
            )
        )
    ]
    barrier = pltpu.get_barrier_semaphore()

    def greet(k, carry):
        pl.semaphore_signal(
            barrier, inc=1, device_id=(lax.rem(n + k, nodes), l), device_id_type=MESH
        )
        return carry

    lax.fori_loop(1, nodes, greet, 0, unroll=nodes <= 16)
    siblings = [(n, lax.rem(l + k, members)) for k in range(1, members)]
    for sibling in siblings:
        pl.semaphore_signal(barrier, inc=1, device_id=sibling, device_id_type=MESH)

    for load in loads[:3]:
        load.start()
    loads[0].wait()
    loads[1].wait()
    ids = ids_ref[...]
    hit = ids % EXPERTS_PER_HOST == 0
    hit_one = jnp.where(hit, 1, 0)
    present = jnp.max(hit_one, 0, keepdims=True)
    dest = jnp.sum(jnp.where(hit, ids // EXPERTS_PER_HOST, 0), 0, keepdims=True)
    dest = jnp.where(present > 0, dest, -1)
    onehot = jnp.where(iota((nodes, tokens), 0) == dest, 1.0, 0.0).astype(f32)
    before = jnp.where(iota((tokens, tokens), 0) < iota((tokens, tokens), 1), 1.0, 0.0)
    earlier = dot(onehot.astype(bf16), before.astype(bf16))
    rank = jnp.sum(onehot * earlier, 0, keepdims=True).astype(jnp.int32)
    key = jnp.where(present > 0, dest * SLAB + rank, -SLAB * CAP)
    matched = jnp.sum(jnp.where(hit, gates_ref[...], 0.0), 0, keepdims=True)
    matched = matched.astype(bf16).astype(f32)

    loads[2].wait()
    for load in loads[3:]:
        load.start()
    place = iota((nodes * SLAB, tokens), 0)

    def pack(q):
        total = None
        for c in range(0, len(plan[q]), 2):
            masks, rights = [], []
            for block in plan[q][c:c + 2]:
                mask = place == key + CAP * (c + len(masks))
                if block is None:
                    masks.append(jnp.where(mask, matched, 0.0).astype(bf16))
                    rights.append(jnp.ones((tokens, WIDTH), bf16))
                else:
                    masks.append(jnp.where(mask, 1.0, 0.0).astype(bf16))
                    rights.append(grads[:, block * WIDTH:(block + 1) * WIDTH])
            part = dot(jnp.concatenate(masks, 1), jnp.concatenate(rights, 0))
            total = part if total is None else total + part
        send[q] = total.astype(bf16).reshape(nodes, SLAB, WIDTH)

    def turn(i):
        return 1 + lax.rem((i + 1) * (nodes // 2 - 1), nodes - 1)

    def push(q):
        def one(i, carry):
            other = lax.rem(n + turn(i), nodes)
            pltpu.make_async_remote_copy(
                src_ref=send.at[q, other], dst_ref=recv.at[q, me],
                send_sem=send_sem.at[q], recv_sem=recv_sem.at[q],
                device_id=(other, l), device_id_type=MESH,
            ).start()
            return carry

        lax.fori_loop(0, nodes - 1, one, 0, unroll=nodes <= 16)
        recv[q, me] = send[q, n]

    def settle(ref, sem):
        pltpu.make_async_copy(ref, ref, sem).wait()

    def relay(q):
        settle(recv.at[q, pl.ds(0, nodes - 1)], recv_sem.at[q])
        mine = recv.at[q, pl.ds(l * nodes, nodes)]
        for sibling in siblings:
            pltpu.make_async_remote_copy(
                src_ref=mine, dst_ref=mine,
                send_sem=pass_send_sem.at[q], recv_sem=pass_recv_sem.at[q],
                device_id=sibling, device_id_type=MESH,
            ).start()

    def collect(q):
        settle(recv.at[q, pl.ds(0, devices - nodes)], pass_recv_sem.at[q])

    def unpack(q, member, scored=False):
        rows = group * CAP
        for g in range(nodes // group):
            source = member * nodes + g * group
            landed = recv[q, pl.ds(source, group)].reshape(group * SLAB, WIDTH)
            chosen = dot(picks[...], landed)
            here = pl.ds(pl.multiple_of(source * CAP, rows), rows)
            local = slice(g * rows, (g + 1) * rows)
            if None in plan[q]:
                c = plan[q].index(None)
                gate[here, :] = chosen[c * rows:(c + 1) * rows]
            factor = gate[here, :]
            sums = None
            for c, block in enumerate(plan[q]):
                if block is None:
                    continue
                part = chosen[c * rows:(c + 1) * rows]
                columns = slice(block * WIDTH, (block + 1) * WIDTH)
                x[here, columns] = part.astype(bf16)
                scaled[here, columns] = (factor * part).astype(bf16)
                if scored:
                    against = back[here, columns].astype(f32)
                    for k in range(members - 1):
                        against += back_parts[k, local, columns].astype(f32)
                    term = part * against
                    sums = term if sums is None else sums + term
            if scored:
                sums = sums[:, :LANES] + sums[:, LANES:]
                score_sums[local, :] = sums if q == 0 else score_sums[local, :] + sums

    def span(q):
        blocks = [b for b in plan[q] if b is not None]
        return blocks[0] * WIDTH, (blocks[-1] + 1) * WIDTH

    def multiply(q):
        first, last = span(q)
        part = dot(weight[:, first:last], x[:, first:last], ((1,), (1,)))
        unscaled[...] = part if q == 0 else unscaled[...] + part

    def decay():
        def tile(i, carry):
            columns = pl.ds(pl.multiple_of(i * WIDTH, WIDTH), WIDTH)
            weight_decayed[:, columns] = weight[:, columns].astype(f32) * (1.0 - learn_rate * decay_rate)
            second_decayed[:, columns] = second[:, columns].astype(f32) * beta_second
            return carry

        lax.fori_loop(0, weight.shape[1] // WIDTH, tile, 0)

    def update(first, last):
        def tile(i, carry):
            columns = pl.ds(pl.multiple_of(i * WIDTH, WIDTH), WIDTH)
            weight_out[:, columns], second_out[:, columns] = adamw(
                hidden_t[...], scaled[:, columns], weight_decayed[:, columns], second_decayed[:, columns]
            )
            return carry

        lax.fori_loop(first, last, tile, 0)

    pack(0)
    pl.semaphore_wait(barrier, nodes - 1 + members - 1)
    push(0)
    for q in range(1, len(plan)):
        pack(q)
        push(q)
    loads[3].wait()
    loads[4].wait()
    features = weight.shape[1]
    stripe = 2 * WIDTH
    for j in range(0, features, stripe):
        back[:, j:j + stripe] = dot(hidden[...], weight[:, j:j + stripe]).astype(back.dtype)
    for k in range(1, members):
        other = lax.rem(l + k, members)
        pltpu.make_async_remote_copy(
            src_ref=back.at[pl.ds(pl.multiple_of(other * half, half), half)], dst_ref=back_parts.at[k - 1],
            send_sem=back_send_sem.at[k - 1], recv_sem=back_recv_sem.at[k - 1],
            device_id=(n, other), device_id_type=MESH,
        ).start()

    picked_row, picked_col = iota((group * CAP, group * SLAB), 0), iota((group * CAP, group * SLAB), 1)
    wanted = (picked_row // CAP) * SLAB + picked_row % CAP
    for c in range(BLOCKS):
        picks[c * group * CAP:(c + 1) * group * CAP, :] = jnp.where(
            picked_col == wanted + CAP * c, 1.0, 0.0
        ).astype(bf16)
    hidden_t[...] = hidden[...].astype(f32).T.astype(bf16)
    loads[5].wait()

    decay()

    for k in range(members - 1):
        settle(back_parts.at[k], back_recv_sem.at[k])
    for q in range(len(plan)):
        relay(q)
        unpack(q, l, scored=True)
        if q == len(plan) - 1:
            for s in range(0, half, LANES):
                part = score_sums[s:min(s + LANES, half), :]
                if part.shape[0] < LANES:
                    part = jnp.concatenate([part, jnp.zeros((LANES - part.shape[0], LANES), f32)], 0)
                score_send[s // LANES] = jnp.sum(part.T, 0, keepdims=True)

            def answer(i, carry):
                other = lax.rem(n + turn(i), nodes)
                pltpu.make_async_remote_copy(
                    src_ref=score_send.at[(CAP * other) // LANES], dst_ref=score_recv.at[n],
                    send_sem=score_send_sem, recv_sem=score_recv_sem,
                    device_id=(other, l), device_id_type=MESH,
                ).start()
                return carry

            lax.fori_loop(0, nodes - 1, answer, 0, unroll=nodes <= 16)
            score_recv[n] = score_send[(CAP * n) // LANES]
        collect(q)
        for k in range(1, members):
            unpack(q, lax.rem(l + k, members))
        multiply(q)
        if q < len(plan) - 1:
            update(early[q], early[q + 1])

    raw = unscaled[...].T
    for j in range(0, units, LANES):
        hidden_out[:, j:j + LANES] = (gate[:, :LANES] * raw[:, j:j + LANES]).astype(bf16)
    update(early[-2], early[-1])

    others = score_recv.at[pl.ds(0, nodes - 1)]
    settle(others, score_recv_sem)
    sums = score_recv[...].reshape(nodes, LANES)
    lane = iota((nodes, LANES), 1) - lax.rem(CAP * n, LANES)
    token_score = jnp.zeros((1, tokens), f32)
    for r in range(CAP):
        column = jnp.sum(jnp.where(lane == r, sums, 0.0), 1, keepdims=True)
        column = jnp.sum(jnp.where(onehot > 0, column, 0.0), 0, keepdims=True)
        token_score += jnp.where(rank == r, column, 0.0)
    score_out[...] = jnp.where(hit, token_score, 0.0)

    settle(others, score_send_sem)
    for k in range(members - 1):
        settle(back_parts.at[k], back_send_sem.at[k])
    for q in range(len(plan)):
        settle(send.at[q, pl.ds(0, nodes - 1)], send_sem.at[q])
        settle(recv.at[q, pl.ds(0, devices - nodes)], pass_send_sem.at[q])


def finish(
    early, scores, hidden_grad, weight, second, weight_decayed, second_decayed, hidden_t, scaled,
    score_out, hidden_out, weight_out, second_out,
    weight_late, second_late, copy_sem,
):
    units, features = weight.shape
    copies = [
        pltpu.make_async_copy(scores, score_out, copy_sem.at[0]),
        pltpu.make_async_copy(hidden_grad, hidden_out, copy_sem.at[1]),
    ]
    pieces = 4
    for i in range(pieces):
        rows = pl.ds(i * (units // pieces), units // pieces)
        for j, (source, target) in enumerate(((weight, weight_out), (second, second_out))):
            copies.append(pltpu.make_async_copy(
                source.at[rows, pl.ds(0, early)], target.at[rows, pl.ds(0, early)],
                copy_sem.at[2 + 2 * i + j],
            ))
    for copy in copies:
        copy.start()
    base = 2 + 2 * pieces
    for i, first in enumerate(range(early, features, WIDTH)):
        columns, late = pl.ds(first, WIDTH), pl.ds(first - early, WIDTH)
        weight_late[:, late], second_late[:, late] = adamw(
            hidden_t[...], scaled[:, columns], weight_decayed[:, columns], second_decayed[:, columns]
        )
        for j, (source, target) in enumerate(((weight_late, weight_out), (second_late, second_out))):
            copies.append(pltpu.make_async_copy(
                source.at[:, late], target.at[:, columns], copy_sem.at[base + 2 * i + j]
            ))
            copies[-1].start()
    for copy in copies:
        copy.wait()


def on_device(nodes, members, grad_out, expert_ids, gate_weights, saved_hidden, down_weight, second_moment):
    tokens, features = grad_out.shape
    _, slots, units = saved_hidden.shape
    chosen = expert_ids.shape[1]
    devices = nodes * members
    group = min(16, nodes)
    half = nodes * CAP
    back_type = f32 if slots * features <= 1 << 20 else bf16
    blocks = [None] + list(range(features // WIDTH))
    plan = [blocks[i:i + BLOCKS] for i in range(0, len(blocks), BLOCKS)]
    chunks = len(plan)
    ahead = features // WIDTH - LATE
    gaps = [0, (4 * ahead) // 7, ahead]
    early = ahead * WIDTH
    small = pl.BlockSpec(memory_space=pltpu.VMEM)
    large = pl.BlockSpec(memory_space=pl.ANY)
    kept = pl.pallas_call(
        functools.partial(kernel, nodes, members, plan, gaps),
        out_shape=(
            pltpu.VMEM((chosen, tokens), f32),
            pltpu.VMEM((slots, units), bf16),
            pltpu.VMEM((units, features), bf16),
            pltpu.VMEM((units, features), bf16),
            pltpu.VMEM((units, features), f32),
            pltpu.VMEM((units, features), f32),
            pltpu.VMEM((units, slots), bf16),
            pltpu.VMEM((slots, features), bf16),
        ),
        in_specs=[large] * 6,
        out_specs=(small,) * 8,
        scratch_shapes=[
            pltpu.VMEM((chosen, tokens), jnp.int32),
            pltpu.VMEM((chosen, tokens), f32),
            pltpu.VMEM((tokens, features), bf16),
            pltpu.VMEM((slots, units), bf16),
            pltpu.VMEM((units, features), bf16),
            pltpu.VMEM((units, features), bf16),
            pltpu.VMEM((chunks, nodes, SLAB, WIDTH), bf16),
            pltpu.VMEM((chunks, devices, SLAB, WIDTH), bf16),
            pltpu.VMEM((BLOCKS * group * CAP, group * SLAB), bf16),
            pltpu.VMEM((slots, features), bf16),
            pltpu.VMEM((slots, WIDTH), f32),
            pltpu.VMEM((units, slots), f32),
            pltpu.VMEM((slots, features), back_type),
            pltpu.VMEM((members - 1, half, features), back_type),
            pltpu.VMEM((half, LANES), f32),
            pltpu.VMEM((-(-half // LANES), 1, LANES), f32),
            pltpu.VMEM((nodes, 1, LANES), f32),
            pltpu.SemaphoreType.DMA((6,)),
            pltpu.SemaphoreType.DMA((chunks,)),
            pltpu.SemaphoreType.DMA((chunks,)),
            pltpu.SemaphoreType.DMA((chunks,)),
            pltpu.SemaphoreType.DMA((chunks,)),
            pltpu.SemaphoreType.DMA((members - 1,)),
            pltpu.SemaphoreType.DMA((members - 1,)),
            pltpu.SemaphoreType.DMA,
            pltpu.SemaphoreType.DMA,
        ],
        compiler_params=pltpu.CompilerParams(
            collective_id=0, has_side_effects=True, vmem_limit_bytes=40 * 1024 * 1024
        ),
        cost_estimate=pl.CostEstimate(
            flops=4 * slots * units * features, bytes_accessed=4 * units * features, transcendentals=0
        ),
    )(expert_ids.T, gate_weights.T, grad_out, saved_hidden[0], down_weight[0], second_moment[0])
    kept = [pltpu.with_memory_space_constraint(a, pltpu.VMEM) for a in kept]
    scores, hidden_grad, new_weight, new_second = pl.pallas_call(
        functools.partial(finish, early),
        out_shape=(
            jax.ShapeDtypeStruct((chosen, tokens), f32),
            jax.ShapeDtypeStruct((slots, units), bf16),
            jax.ShapeDtypeStruct((units, features), bf16),
            jax.ShapeDtypeStruct((units, features), bf16),
        ),
        in_specs=[small] * 8,
        out_specs=(large,) * 4,
        scratch_shapes=[
            pltpu.VMEM((units, features - early), bf16),
            pltpu.VMEM((units, features - early), bf16),
            pltpu.SemaphoreType.DMA((10 + 2 * LATE,)),
        ],
        compiler_params=pltpu.CompilerParams(vmem_limit_bytes=16 * 1024 * 1024),
        cost_estimate=pl.CostEstimate(
            flops=2 * slots * units * LATE * WIDTH, bytes_accessed=4 * units * features, transcendentals=0
        ),
    )(*kept)
    return scores.T, hidden_grad[None], new_weight[None], new_second[None]


def solution(mesh):
    return jax.shard_map(
        functools.partial(on_device, mesh.shape["node"], mesh.shape["local"]),
        mesh=mesh,
        in_specs=(
            P(("node", "local"), None),
            P(("node", "local"), None),
            P(("node", "local"), None),
            P("node", None, "local"),
            P("node", "local", None),
            P("node", "local", None),
        ),
        out_specs=(
            P(("node", "local"), None),
            P("node", None, "local"),
            P("node", "local", None),
            P("node", "local", None),
        ),
        check_vma=False,
    )
```
